32 devices in a mesh: cells: 8 (over z, x), bands: 4 (over y, core).
Axes of the slice: x: 2, y: 2, z: 4, core: 2. Of those that a mesh axis runs over, the one named last changes fastest.
Arguments:
- wavefunctions: bfloat16 [5832, 512], P('cells', 'bands'), may hold values from -6 to 6
- hamiltonians: bfloat16 [8, 729, 729], P('cells'), may hold values from -0.21875 to 0.21875
- connectivity: int32 [8, 729], P('cells'), may hold values from 0 to 728, as said below
- face_nodes: int32 [16, 81], P('cells'), may hold values from 0 to 728, as said below
Outputs:
- filtered: float32 [5832, 512], P('cells', 'bands')
- correlation: float32 [512, 512], P(None, 'bands')
The draws below stay inside these ranges and needn't reach their ends.
Inputs may be any that keep to these rules, and one draw needn't show every extreme that they name: `connectivity`: within each partition the values are a permutation of the local node numbers laid on a lattice: cell c's node (i, j, k), 0 <= i, j, k <= 8, is lattice point (8 c + i, j, k) of the partition, so consecutive cells of a partition share 81 nodes and every local node belongs to some cell. `face_nodes`: row 0 of a partition lists the local numbers of its lattice points with first coordinate 0, row 1 those with first coordinate 8, in the order of the other two coordinates; neighbouring partitions list the same physical face nodes in the same order.
All inputs are finite; a program needn't handle non-finite values.
Results may differ from the reference program's by a relative error of at most 0.0039.
Values may be sent and summed in bfloat16 or wider, within the bound.
No kernel may reach another device: no remote copies, remote signals or barrier semaphores. Data moves between devices by JAX's collectives and lax.ppermute only.
A program may use at most 64 MiB of HBM per device.

```python
import jax
import jax.numpy as jnp
from jax import lax

ORDER = 8
STEPS = 2
CELL_NODES = 729
SHARED = 81
CELLS_DEV = 1
NODES_DEV = 729
PARTITIONS = 8
BANDS = 512


def node_permutations(key):
    base_key = jax.random.fold_in(key, 11)
    part_keys = jax.vmap(lambda position: jax.random.fold_in(base_key, position))(jnp.arange(PARTITIONS, dtype=jnp.int32))
    return jax.vmap(lambda part_key: jax.random.permutation(part_key, NODES_DEV))(part_keys).astype(jnp.int32)


def draw_connectivity(key, part):
    node_perms = node_permutations(key)
    cell_ids = jnp.arange(CELLS_DEV, dtype=jnp.int32)[:, None]
    local_ids = jnp.arange(CELL_NODES, dtype=jnp.int32)[None, :]
    layer_x = local_ids // SHARED
    plane_pos = local_ids % SHARED
    lattice = (ORDER * cell_ids + layer_x) * SHARED + plane_pos
    return node_perms[:, lattice].reshape(PARTITIONS * CELLS_DEV, CELL_NODES).astype(jnp.int32)


def draw_face_nodes(key, part):
    node_perms = node_permutations(key)
    low_face = node_perms[:, :SHARED]
    high_face = node_perms[:, ORDER * CELLS_DEV * SHARED:]
    return jnp.stack([low_face, high_face], axis=1).reshape(PARTITIONS * 2, SHARED).astype(jnp.int32)


def shard_levels(own_key, shape, pieces, least, high):
    level = 1.0
    for axis_at, blocks in pieces:
        draws = jax.random.uniform(jax.random.fold_in(jax.random.fold_in(own_key, 6), axis_at), (blocks,), jnp.float32, least / len(pieces), high / len(pieces))
        level = level * jnp.repeat(jnp.exp(draws), shape[axis_at] // blocks).reshape((-1,) + (1,) * (len(shape) - 1 - axis_at))
    return level


def gaussian(key, extent, width, bound, pieces=(), held_as=jnp.bfloat16):
    loudness = shard_levels(key, extent, pieces, -0.22, 0.18) if pieces else 1.0
    values = jax.random.normal(key, extent, jnp.float32) * width * loudness
    return jnp.minimum(jnp.maximum(values, -bound), bound).astype(held_as)


def setup_inputs(seed: int = 0) -> dict:
    key_list = jax.random.split(jax.random.key(seed), 5)
    return {
        "wavefunctions": gaussian(key_list[0], (PARTITIONS * NODES_DEV, BANDS), 1.0, 6.0, ((0, 8), (1, 4))),
        "hamiltonians": gaussian(key_list[1], (PARTITIONS * CELLS_DEV, CELL_NODES, CELL_NODES), CELL_NODES ** -0.5, 0.21875, ((0, 8),)),
        "connectivity": draw_connectivity(jax.random.fold_in(key_list[4], 71), 0),
        "face_nodes": draw_face_nodes(jax.random.fold_in(key_list[4], 71), 0),
    }


def apply_local(vector_bf, cell_hams, cell_nodes):
    def one_part(entries):
        values, hams_part, nodes_part = entries
        gathered = values[nodes_part].astype(jnp.float32)
        cell_terms = jnp.einsum('cij,cjb->cib', hams_part.astype(jnp.float32), gathered, precision=lax.Precision.HIGHEST)
        summed = jnp.zeros((NODES_DEV, BANDS), jnp.float32)
        return summed.at[nodes_part.reshape(-1)].add(cell_terms.reshape(-1, BANDS))
    return lax.map(one_part, (vector_bf, cell_hams, cell_nodes))


def assemble(local_sums, face_index):
    face_vals = jax.vmap(lambda values, rows: values[rows])(local_sums, face_index)
    zero_face = jnp.zeros((1, SHARED, BANDS), jnp.float32)
    from_before = jnp.concatenate([zero_face, face_vals[:-1, 1]], axis=0)
    from_after = jnp.concatenate([face_vals[1:, 0], zero_face], axis=0)

    def add_faces(values, rows, before, after):
        return values.at[rows[0]].add(before).at[rows[1]].add(after)
    return jax.vmap(add_faces)(local_sums, face_index, from_before, from_after)


def reference(wavefunctions, hamiltonians, connectivity, face_nodes):
    start_vec = wavefunctions.reshape(PARTITIONS, NODES_DEV, BANDS).astype(jnp.float32)
    cell_hams = hamiltonians.reshape(PARTITIONS, CELLS_DEV, CELL_NODES, CELL_NODES)
    cell_nodes = connectivity.reshape(PARTITIONS, CELLS_DEV, CELL_NODES)
    face_index = face_nodes.reshape(PARTITIONS, 2, SHARED)

    def operate(vector):
        return assemble(apply_local(vector.astype(jnp.bfloat16), cell_hams, cell_nodes), face_index)

    older = start_vec
    newer = 0.5 * operate(start_vec)
    for step in range(STEPS - 1):
        following = operate(newer) - older
        older = newer
        newer = following
    filtered = newer.reshape(PARTITIONS * NODES_DEV, BANDS)

    def keep_part(position, rows):
        value = jnp.where(position > 0, jnp.float32(0.0), jnp.float32(1.0))
        return jnp.ones((NODES_DEV,), jnp.float32).at[rows].set(value)
    keep_rows = jax.vmap(keep_part)(jnp.arange(PARTITIONS, dtype=jnp.int32), face_index[:, 0])
    masked = newer * keep_rows[:, :, None]

    def add_part(gram_sum, values):
        high_word = values.astype(jnp.bfloat16)
        term = jnp.dot(high_word.T, high_word, preferred_element_type=jnp.float32)
        return gram_sum + term, None

    gram, unused = lax.scan(add_part, jnp.zeros((BANDS, BANDS), jnp.float32), masked)
    correlation = gram / (PARTITIONS * NODES_DEV)
    return filtered, correlation
```

```python
import jax
import jax.numpy as jnp
from jax import lax
from jax.sharding import PartitionSpec as P

BF16 = jnp.bfloat16
F32 = jnp.float32


def digits(count):
    stride, left, out = 1, count, []
    for radix in range(2, count + 1):
        while left % radix == 0:
            out.append((stride, radix))
            stride *= radix
            left //= radix
    return out


def turned(count, stride, radix, by):
    pairs = []
    for source in range(count):
        digit = source // stride % radix
        pairs.append((source, source + ((digit + by) % radix - digit) * stride))
    return pairs


def sum_over(axis, value):
    count = lax.axis_size(axis)
    for stride, radix in digits(count):
        word = value.astype(BF16)
        value = word.astype(F32)
        for by in range(1, radix):
            value = value + lax.ppermute(word, axis, turned(count, stride, radix, by)).astype(F32)
    return value


def gather_over(axis, own):
    count = lax.axis_size(axis)
    blocks = {0: own}
    for stride, radix in reversed(digits(count)):
        for at, block in list(blocks.items()):
            for by in range(1, radix):
                blocks[at + by * stride] = lax.ppermute(block, axis, turned(count, stride, radix, radix - by))
    return blocks


def one_hot_t(flags, values):
    return lax.dot_general(flags, values, (((0,), (0,)), ((), ())), preferred_element_type=F32)


def body(wavefunctions, hamiltonians, connectivity, face_nodes):
    node_count, width = wavefunctions.shape
    shared = face_nodes.shape[1]
    place = lax.axis_index("cells")
    parts = lax.axis_size("cells")
    hamiltonian = hamiltonians[0]
    cell = connectivity[0]
    place_of = (lax.broadcasted_iota(jnp.int32, (node_count, node_count), 0) == cell[None, :]).astype(BF16)
    face = (face_nodes.reshape(-1)[:, None] == cell[None, :]).astype(BF16)
    start = one_hot_t(place_of, wavefunctions)
    ahead = [(i, (i + 1) % parts) for i in range(parts)]
    back = [((i + 1) % parts, i) for i in range(parts)]

    def halo(sums):
        rows = jnp.dot(face, sums.astype(BF16), preferred_element_type=F32).astype(BF16)
        before = lax.ppermute(rows[shared:], "cells", ahead)
        after = lax.ppermute(rows[:shared], "cells", back)
        before = jnp.where(place > 0, before, jnp.zeros_like(before))
        after = jnp.where(place < parts - 1, after, jnp.zeros_like(after))
        return one_hot_t(face, jnp.concatenate([before, after]))

    local = jnp.dot(hamiltonian, start.astype(BF16), preferred_element_type=F32)
    newer = 0.5 * (local + halo(local))
    local = jnp.dot(hamiltonian, newer.astype(BF16), preferred_element_type=F32)
    following = local + halo(local) - start

    top = following.astype(BF16)
    rest = following - top.astype(F32)
    middle = rest.astype(BF16)
    low = (rest - middle.astype(F32)).astype(BF16)
    filtered = sum(jnp.dot(place_of, word, preferred_element_type=F32) for word in (low, middle, top))

    first_face = jnp.sum(face[:shared].astype(F32), axis=0)
    keep = jnp.where(place > 0, 1.0 - first_face, jnp.ones_like(first_face))
    word = (following * keep[:, None]).astype(BF16)
    groups = lax.axis_size("bands")
    blocks = gather_over("bands", word)
    gram = jnp.stack([one_hot_t(blocks[turn], word) for turn in range(groups)])
    total = sum_over("cells", gram)
    group = lax.axis_index("bands")
    order = jnp.zeros((groups,), jnp.int32)
    for stride, radix in digits(groups):
        at = jnp.arange(groups, dtype=jnp.int32) // stride % radix
        order = order + (at - group // stride % radix) % radix * stride
    correlation = total[order].reshape(groups * width, width) / (parts * node_count)
    return filtered, correlation


def solution(mesh):
    placed = (P("cells", "bands"), P("cells", None, None), P("cells", None), P("cells", None))
    return jax.shard_map(
        body,
        mesh=mesh,
        in_specs=placed,
        out_specs=(P("cells", "bands"), P(None, "bands")),
        check_vma=False,
    )
```

```python
import jax
import jax.numpy as jnp
from jax import lax
from jax.experimental import pallas as pl
from jax.experimental.pallas import tpu as pltpu
from jax.sharding import PartitionSpec as P

BF16 = jnp.bfloat16
F32 = jnp.float32


def digits(count):
    stride, left, out = 1, count, []
    for radix in range(2, count + 1):
        while left % radix == 0:
            out.append((stride, radix))
            stride *= radix
            left //= radix
    return out


def turn(index, stride, radix, by):
    digit = index // stride % radix
    return index + ((digit + by) % radix - digit) * stride


def turned(count, stride, radix, by):
    return [(source, turn(source, stride, radix, by)) for source in range(count)]


def sum_over(axis, value):
    count = lax.axis_size(axis)
    for stride, radix in digits(count):
        word = value.astype(BF16)
        value = word.astype(F32)
        for by in range(1, radix):
            value = value + lax.ppermute(word, axis, turned(count, stride, radix, by)).astype(F32)
    return value


def dot(a, b):
    return jnp.dot(a, b, preferred_element_type=F32)


def dot_t(a, b):
    return lax.dot_general(a, b, (((0,), (0,)), ((), ())), preferred_element_type=F32)


def one_hot(flags):
    return jnp.where(flags, jnp.float32(1), jnp.float32(0)).astype(BF16)


def first_kernel(waves_hbm, cell_hbm, faces_hbm, ham_hbm, start, local, sums, ham, one, columns, waves, cell, faces, rows, sems):
    pairs = ((cell_hbm, cell), (faces_hbm, faces), (waves_hbm, waves), (ham_hbm.at[0], ham))
    copies = [pltpu.make_async_copy(source, target, sems.at[at]) for at, (source, target) in enumerate(pairs)]
    for copy in copies:
        copy.start()
    count = waves.shape[0]
    shared = faces.shape[1]
    padded = one.shape[0] // 2
    rows[...] = jnp.full(rows.shape, -1, F32)
    copies[0].wait()
    copies[1].wait()
    row = cell[...].astype(F32)
    rows[0:1, :count] = row
    rows[1:3, :shared] = faces[...].astype(F32)
    turned_rows = jnp.transpose(rows[...])
    columns[...] = turned_rows
    nodes = lax.broadcasted_iota(jnp.int32, (count, count), 1).astype(F32)
    place = one_hot(turned_rows[:count, 0:1] == nodes)
    pick = one_hot(jnp.concatenate([turned_rows[:padded, 1:2], turned_rows[:padded, 2:3]], axis=0) == row)
    one[...] = pick
    copies[2].wait()
    begin = dot(place, waves[...]).astype(BF16)
    start[...] = begin
    copies[3].wait()
    result = dot(ham[...], begin)
    local[...] = result
    sums[...] = dot(pick, result.astype(BF16)).astype(BF16)


def middle_kernel(ends, columns, faces, one_t, keep):
    count = one_t.shape[0]
    shared = faces.shape[1]
    padded = one_t.shape[1] // 2
    col = columns[:count, 0:1]
    row = faces[...].astype(F32)
    has_before = jnp.where(ends[0] > 0, jnp.float32(1), jnp.float32(0))
    has_after = jnp.where(ends[1] > 0, jnp.float32(1), jnp.float32(0))
    first = jnp.where(col == row[0:1], jnp.float32(1), jnp.float32(0))
    second = jnp.where(col == row[1:2], jnp.float32(1), jnp.float32(0))
    one_t[...] = jnp.zeros(one_t.shape, BF16)
    one_t[:, :shared] = (first * has_before).astype(BF16)
    one_t[:, padded : padded + shared] = (second * has_after).astype(BF16)
    on_first = jnp.sum(first, axis=1, keepdims=True) * has_before
    on_second = jnp.sum(second, axis=1, keepdims=True)
    keep[...] = jnp.broadcast_to(1.0 - on_first - on_second, keep.shape)


def second_kernel(local, before, after, ham, start, one, one_t, keep, partial, block, sums):
    count = local.shape[0]
    padded = before.shape[0]
    head = block.shape[0] - padded
    halo = jnp.concatenate([before[...], after[...]], axis=0)
    newer = 0.5 * (local[...] + dot(one_t[...], halo))
    result = dot(ham[...], newer.astype(BF16))
    rest = result - start[...].astype(F32)
    partial[...] = rest
    sums[...] = dot(one[...], result.astype(BF16)).astype(BF16)
    block[count:head, :] = jnp.zeros((head - count, block.shape[1]), BF16)
    block[:count, :] = (rest * keep[...]).astype(BF16)
    block[head:, :] = dot(one[padded:, :], rest.astype(BF16)).astype(BF16)


def vmem(count):
    return [pl.BlockSpec(memory_space=pltpu.VMEM)] * count


def body(wavefunctions, hamiltonians, connectivity, face_nodes):
    node_count, width = wavefunctions.shape
    shared = face_nodes.shape[1]
    padded = -(-shared // 32) * 32
    head = -(-node_count // 16) * 16
    lanes = -(-node_count // 128) * 128
    parts = lax.axis_size("cells")
    groups = lax.axis_size("bands")
    place = lax.axis_index("cells")
    group = lax.axis_index("bands")
    nodal = (node_count, width)
    shape = jax.ShapeDtypeStruct
    params = pltpu.CompilerParams(vmem_limit_bytes=24 * 2**20)

    start, local, sums, ham, one, columns = pl.pallas_call(
        first_kernel,
        out_shape=(
            shape(nodal, BF16),
            shape(nodal, F32),
            shape((2 * padded, width), BF16),
            shape(hamiltonians.shape[1:], BF16),
            shape((2 * padded, node_count), BF16),
            shape((lanes, 8), F32),
        ),
        in_specs=[pl.BlockSpec(memory_space=pltpu.HBM)] * 4,
        out_specs=tuple(vmem(6)),
        scratch_shapes=[
            pltpu.VMEM(nodal, BF16),
            pltpu.VMEM(connectivity.shape, jnp.int32),
            pltpu.VMEM(face_nodes.shape, jnp.int32),
            pltpu.VMEM((8, lanes), F32),
            pltpu.SemaphoreType.DMA((4,)),
        ],
        compiler_params=params,
    )(*(pltpu.with_memory_space_constraint(x, pltpu.HBM) for x in (wavefunctions, connectivity, face_nodes, hamiltonians)))

    both = ("cells", "bands")
    stride, radix = digits(groups)[-1] if groups > 1 else (1, 1)

    def pair_swap(first):
        pairs = []
        for part in range(parts):
            other = first + ((part - first) ^ 1)
            for band in range(groups):
                if part >= first and other < parts:
                    pairs.append((part * groups + band, other * groups + band))
                else:
                    pairs.append((part * groups + band, part * groups + turn(band, stride, radix, 1)))
        return pairs

    odd = place % 2 == 1

    def neighbours(sums):
        low, high = sums[:padded], sums[padded:]
        even_odd = lax.ppermute(jnp.where(odd, low, high), both, pair_swap(0))
        odd_even = lax.ppermute(jnp.where(odd, high, low), both, pair_swap(1))
        return jnp.where(odd, even_odd, odd_even), jnp.where(odd, odd_even, even_odd)

    before, after = neighbours(sums)
    ends = jnp.stack([place, parts - 1 - place]).astype(jnp.int32)
    one_t, keep = pl.pallas_call(
        middle_kernel,
        out_shape=(shape((node_count, 2 * padded), BF16), shape(nodal, F32)),
        in_specs=[pl.BlockSpec(memory_space=pltpu.SMEM)] + vmem(2),
        out_specs=tuple(vmem(2)),
        compiler_params=params,
    )(ends, columns, face_nodes)
    partial, block, sums = pl.pallas_call(
        second_kernel,
        out_shape=(shape(nodal, F32), shape((head + padded, width), BF16), shape((2 * padded, width), BF16)),
        in_specs=vmem(8),
        out_specs=tuple(vmem(3)),
        compiler_params=params,
    )(local, before, after, ham, start, one, one_t, keep)

    blocks = {0: block}
    tails = {}
    for stride, radix in digits(groups)[1:]:
        for at in list(blocks):
            for by in range(1, radix):
                blocks[at + by * stride] = lax.ppermute(blocks[at], "bands", turned(groups, stride, radix, radix - by))
    before, after = neighbours(sums)
    has_after = place < parts - 1
    tails[0] = after
    for at in list(blocks)[1:]:
        pairs = []
        for part in range(parts):
            for band in range(groups):
                target = band
                for stride, radix in digits(groups)[1:]:
                    target = turn(target, stride, radix, radix - at // stride % radix)
                pairs.append((part * groups + band, (part - 1) % parts * groups + target))
        tails[at] = lax.ppermute(sums[:padded], both, pairs)
    for at in list(blocks):
        tail = jnp.where(has_after, tails[at], jnp.zeros_like(tails[at]))
        blocks[at] = blocks[at].at[head:].add(tail)
    for stride, radix in digits(groups)[:1]:
        for at in list(blocks):
            for by in range(1, radix):
                blocks[at + by * stride] = lax.ppermute(blocks[at], "bands", turned(groups, stride, radix, radix - by))
    gram = jnp.stack([dot_t(blocks[at], blocks[0]) for at in range(groups)])
    gram, partial, before, after = lax.optimization_barrier((gram, partial, before, after))
    total = sum_over("cells", gram) * (1.0 / (parts * node_count))
    radices = digits(groups)
    total = total.reshape(tuple(radix for _, radix in reversed(radices)) + (width, width))
    for at, (stride, radix) in enumerate(radices):
        digit = group // stride % radix
        moved = total
        for by in range(1, radix):
            moved = jnp.where(digit == by, jnp.roll(total, by, axis=len(radices) - 1 - at), moved)
        total = moved
    correlation = total.reshape(groups * width, width)

    before = jnp.where(place > 0, before, jnp.zeros_like(before))[:shared]
    after = jnp.where(has_after, after, jnp.zeros_like(after))[:shared]
    nodes = lax.broadcasted_iota(jnp.int32, (node_count, node_count), 0)
    place_of = (nodes == connectivity).astype(BF16)
    face_of = (face_nodes.reshape(-1)[None, :] == nodes[:, :1]).astype(BF16)
    top = partial.astype(BF16)
    rest = partial - top.astype(F32)
    middle = rest.astype(BF16)
    small = (rest - middle.astype(F32)).astype(BF16)
    halo = jnp.concatenate([before, after])
    filtered = dot(place_of, small) + dot(place_of, middle) + dot(face_of, halo) + dot(place_of, top)
    return filtered, correlation


def solution(mesh):
    placed = (P("cells", "bands"), P("cells", None, None), P("cells", None), P("cells", None))
    return jax.shard_map(
        body,
        mesh=mesh,
        in_specs=placed,
        out_specs=(P("cells", "bands"), P(None, "bands")),
        check_vma=False,
    )
```

```python
import jax
import jax.numpy as jnp
from jax import lax
from jax.experimental import pallas as pl
from jax.experimental.pallas import tpu as pltpu
from jax.sharding import PartitionSpec as P

BF16 = jnp.bfloat16
F32 = jnp.float32


def digits(count):
    stride, left, out = 1, count, []
    for radix in range(2, count + 1):
        while left % radix == 0:
            out.append((stride, radix))
            stride *= radix
            left //= radix
    return out


def turn(index, stride, radix, by):
    digit = index // stride % radix
    return index + ((digit + by) % radix - digit) * stride


def turned(count, stride, radix, by):
    return [(source, turn(source, stride, radix, by)) for source in range(count)]


def sum_over_cells(value):
    parts, groups = lax.axis_size("cells"), lax.axis_size("bands")
    binary = [stride for stride, radix in digits(parts) if radix == 2]
    other = [(stride, radix) for stride, radix in digits(parts) if radix != 2]
    masks = [stride + (stride // 2 if stride > 2 else 0) for stride in binary]
    steps = [[(mask, masks[at - 1])] for at, mask in enumerate(masks)]
    steps = [[lambda part, band, m=m: part ^ m[band % 2] for m in step] for step in steps]
    for stride, radix in other:
        steps.append([lambda part, band, d=(stride, radix, by): turn(part, *d) for by in range(1, radix)])
    for step in steps:
        word = value.astype(BF16)
        value = word.astype(F32)
        for move in step:
            pairs = [
                (part * groups + band, move(part, band) * groups + band) for part in range(parts) for band in range(groups)
            ]
            value = value + lax.ppermute(word, ("cells", "bands"), pairs).astype(F32)
    return value


def dot(a, b):
    return jnp.dot(a, b, preferred_element_type=F32)


def dot_t(a, b):
    return lax.dot_general(a, b, (((0,), (0,)), ((), ())), preferred_element_type=F32)


def one_hot(flags):
    return jnp.where(flags, jnp.float32(1), jnp.float32(0)).astype(BF16)


def row_chunks(count):
    return [(first, min(first + 256, count)) for first in range(0, count, 256)]


def tall_dot(rows_of, values):
    return jnp.concatenate([dot(rows_of(first, last), values) for first, last in row_chunks(values.shape[0])], axis=0)


def first_kernel(waves_hbm, cell_hbm, faces_hbm, ham_hbm, start, local, sums, ham, one, columns, waves, cell, faces, rows, sems):
    count = waves.shape[0]
    shared = faces.shape[1]
    padded = one.shape[0] // 2
    chunks = row_chunks(count)
    pairs = [(cell_hbm, cell), (faces_hbm, faces), (waves_hbm, waves)]
    pairs += [(ham_hbm.at[0, first:last], ham.at[first:last]) for first, last in chunks]
    copies = [pltpu.make_async_copy(source, target, sems.at[at]) for at, (source, target) in enumerate(pairs)]
    for copy in copies:
        copy.start()
    rows[...] = jnp.full(rows.shape, -1, F32)
    copies[0].wait()
    copies[1].wait()
    row = cell[...].astype(F32)
    rows[0:1, :count] = row
    rows[1:3, :shared] = faces[...].astype(F32)
    turned_rows = jnp.transpose(rows[...])
    columns[...] = turned_rows
    nodes = lax.broadcasted_iota(jnp.int32, (count, count), 1).astype(F32)
    place = one_hot(turned_rows[:count, 0:1] == nodes)
    pick = one_hot(jnp.concatenate([turned_rows[:padded, 1:2], turned_rows[:padded, 2:3]], axis=0) == row)
    one[...] = pick
    copies[2].wait()
    begin = tall_dot(lambda first, last: place[first:last], waves[...]).astype(BF16)
    start[...] = begin
    for at, (first, last) in enumerate(chunks):
        copies[3 + at].wait()
        local[first:last] = dot(ham[first:last], begin)
    sums[...] = dot(pick, local[...].astype(BF16)).astype(BF16)


def middle_kernel(ends, columns, faces, one_t, keep):
    count = one_t.shape[0]
    shared = faces.shape[1]
    padded = one_t.shape[1] // 2
    col = columns[:count, 0:1]
    row = faces[...].astype(F32)
    has_before = jnp.where(ends[0] > 0, jnp.float32(1), jnp.float32(0))
    has_after = jnp.where(ends[1] > 0, jnp.float32(1), jnp.float32(0))
    first = jnp.where(col == row[0:1], jnp.float32(1), jnp.float32(0))
    second = jnp.where(col == row[1:2], jnp.float32(1), jnp.float32(0))
    one_t[...] = jnp.zeros(one_t.shape, BF16)
    one_t[:, :shared] = (first * has_before).astype(BF16)
    one_t[:, padded : padded + shared] = (second * has_after).astype(BF16)
    on_first = jnp.sum(first, axis=1, keepdims=True) * has_before
    on_second = jnp.sum(second, axis=1, keepdims=True)
    keep[...] = jnp.broadcast_to(1.0 - on_first - on_second, keep.shape)


def second_kernel(local, before, after, ham, start, one, one_t, keep, partial, block, sums):
    count = local.shape[0]
    padded = before.shape[0]
    head = block.shape[0] - padded
    halo = jnp.concatenate([before[...], after[...]], axis=0)
    newer = 0.5 * (local[...] + dot(one_t[...], halo))
    width = local.shape[1]
    result = tall_dot(lambda first, last: ham[first:last], newer.astype(BF16))
    rest = result - start[...].astype(F32)
    partial[...] = rest
    on_faces = dot(one[...], jnp.concatenate([result.astype(BF16), rest.astype(BF16)], axis=1)).astype(BF16)
    sums[...] = on_faces[:, :width]
    block[count:head, :] = jnp.zeros((head - count, width), BF16)
    block[:count, :] = (rest * keep[...]).astype(BF16)
    block[head:, :] = on_faces[padded:, width:]


def vmem(count):
    return [pl.BlockSpec(memory_space=pltpu.VMEM)] * count


def body(wavefunctions, hamiltonians, connectivity, face_nodes):
    node_count, width = wavefunctions.shape
    shared = face_nodes.shape[1]
    padded = -(-shared // 32) * 32
    head = -(-node_count // 16) * 16
    lanes = -(-node_count // 128) * 128
    parts = lax.axis_size("cells")
    groups = lax.axis_size("bands")
    place = lax.axis_index("cells")
    group = lax.axis_index("bands")
    nodal = (node_count, width)
    shape = jax.ShapeDtypeStruct
    params = pltpu.CompilerParams(vmem_limit_bytes=24 * 2**20)

    start, local, sums, ham, one, columns = pl.pallas_call(
        first_kernel,
        out_shape=(
            shape(nodal, BF16),
            shape(nodal, F32),
            shape((2 * padded, width), BF16),
            shape(hamiltonians.shape[1:], BF16),
            shape((2 * padded, node_count), BF16),
            shape((lanes, 8), F32),
        ),
        in_specs=[pl.BlockSpec(memory_space=pltpu.HBM)] * 4,
        out_specs=tuple(vmem(6)),
        scratch_shapes=[
            pltpu.VMEM(nodal, BF16),
            pltpu.VMEM(connectivity.shape, jnp.int32),
            pltpu.VMEM(face_nodes.shape, jnp.int32),
            pltpu.VMEM((8, lanes), F32),
            pltpu.SemaphoreType.DMA((3 + len(row_chunks(node_count)),)),
        ],
        compiler_params=params,
    )(*(pltpu.with_memory_space_constraint(x, pltpu.HBM) for x in (wavefunctions, connectivity, face_nodes, hamiltonians)))

    both = ("cells", "bands")
    stride, radix = digits(groups)[-1] if groups > 1 else (1, 1)

    def pair_swap(first):
        pairs = []
        for part in range(parts):
            other = first + ((part - first) ^ 1)
            for band in range(groups):
                if part >= first and other < parts:
                    pairs.append((part * groups + band, other * groups + band))
                else:
                    pairs.append((part * groups + band, part * groups + turn(band, stride, radix, 1)))
        return pairs

    odd = place % 2 == 1

    def neighbours(sums):
        low, high = sums[:padded], sums[padded:]
        even_odd = lax.ppermute(jnp.where(odd, low, high), both, pair_swap(0))
        odd_even = lax.ppermute(jnp.where(odd, high, low), both, pair_swap(1))
        return jnp.where(odd, even_odd, odd_even), jnp.where(odd, odd_even, even_odd)

    before, after = neighbours(sums)
    ends = jnp.stack([place, parts - 1 - place]).astype(jnp.int32)
    one_t, keep = pl.pallas_call(
        middle_kernel,
        out_shape=(shape((node_count, 2 * padded), BF16), shape(nodal, F32)),
        in_specs=[pl.BlockSpec(memory_space=pltpu.SMEM)] + vmem(2),
        out_specs=tuple(vmem(2)),
        compiler_params=params,
    )(ends, columns, face_nodes)
    partial, block, sums = pl.pallas_call(
        second_kernel,
        out_shape=(shape(nodal, F32), shape((head + padded, width), BF16), shape((2 * padded, width), BF16)),
        in_specs=vmem(8),
        out_specs=tuple(vmem(3)),
        compiler_params=params,
    )(local, before, after, ham, start, one, one_t, keep)

    core, chips = digits(groups)[:1], digits(groups)[1:]
    low = sums[:padded]
    has_after = place < parts - 1
    blocks = {0: block}
    for stride, radix in chips:
        for at in list(blocks):
            for by in range(1, radix):
                blocks[at + by * stride] = lax.ppermute(blocks[at], "bands", turned(groups, stride, radix, radix - by))
    raw = {}
    for stride, radix in core:
        for by in range(1, radix):
            raw[by * stride] = lax.ppermute(block, "bands", turned(groups, stride, radix, radix - by))
    before, after = neighbours(sums)
    tails = {0: jnp.where(has_after, after, jnp.zeros_like(after))}
    blocks[0] = blocks[0].at[head:].add(tails[0])
    for at in list(blocks)[1:]:
        pairs = []
        for part in range(parts):
            for band in range(groups):
                target = band
                for stride, radix in chips:
                    target = turn(target, stride, radix, radix - at // stride % radix)
                pairs.append((part * groups + band, (part - 1) % parts * groups + target))
        tail = lax.ppermute(low, both, pairs)
        tails[at] = jnp.where(has_after, tail, jnp.zeros_like(tail))
        blocks[at] = blocks[at].at[head:].add(tails[at])
    after = tails[0]
    relayed = jnp.concatenate([after] + [blocks[at] for at in list(blocks)[1:]])
    for stride, radix in core:
        for by in range(1, radix):
            got = lax.ppermute(relayed, "bands", turned(groups, stride, radix, radix - by))
            raw[by * stride] = raw[by * stride].at[head:].add(got[:padded])
            for place_at, at in enumerate(list(blocks)[1:]):
                first = padded + place_at * block.shape[0]
                raw[at + by * stride] = got[first : first + block.shape[0]]
    blocks.update(raw)
    gram = jnp.stack([dot_t(blocks[at], blocks[0]) for at in range(groups)])

    gram, partial, before, after = lax.optimization_barrier((gram, partial, before, after))
    total = sum_over_cells(gram) * (1.0 / (parts * node_count))
    before = jnp.where(place > 0, before, jnp.zeros_like(before))
    radices = digits(groups)
    total = total.reshape(tuple(radix for _, radix in reversed(radices)) + (width, width))
    for at, (stride, radix) in enumerate(radices):
        digit = group // stride % radix
        moved = total
        for by in range(1, radix):
            moved = jnp.where(digit == by, jnp.roll(total, by, axis=len(radices) - 1 - at), moved)
        total = moved
    correlation = total.reshape(groups * width, width)

    nodes = lax.broadcasted_iota(jnp.int32, (node_count, node_count), 0)
    place_of = (nodes == connectivity).astype(BF16)
    face_of = (face_nodes.reshape(-1)[None, :] == nodes[:, :1]).astype(BF16)
    top = partial.astype(BF16)
    rest = partial - top.astype(F32)
    middle = rest.astype(BF16)
    small = (rest - middle.astype(F32)).astype(BF16)
    halo = jnp.concatenate([before[:shared], after[:shared]])
    filtered = dot(place_of, small) + dot(place_of, middle) + dot(face_of, halo) + dot(place_of, top)
    return filtered, correlation


def solution(mesh):
    placed = (P("cells", "bands"), P("cells", None, None), P("cells", None), P("cells", None))
    return jax.shard_map(
        body,
        mesh=mesh,
        in_specs=placed,
        out_specs=(P("cells", "bands"), P(None, "bands")),
        check_vma=False,
    )
```

```python
import jax
import jax.numpy as jnp
from jax import lax
from jax.experimental import pallas as pl
from jax.experimental.pallas import tpu as pltpu
from jax.sharding import PartitionSpec as P

BF16 = jnp.bfloat16
F32 = jnp.float32


def digits(count):
    stride, left, out = 1, count, []
    for radix in range(2, count + 1):
        while left % radix == 0:
            out.append((stride, radix))
            stride *= radix
            left //= radix
    return out


def turn(index, stride, radix, by):
    digit = index // stride % radix
    return index + ((digit + by) % radix - digit) * stride


def turned(count, stride, radix, by):
    return [(source, turn(source, stride, radix, by)) for source in range(count)]


def sum_over_cells(value):
    parts, groups = lax.axis_size("cells"), lax.axis_size("bands")
    binary = [stride for stride, radix in digits(parts) if radix == 2]
    other = [(stride, radix) for stride, radix in digits(parts) if radix != 2]
    masks = [stride + (stride // 2 if stride > 2 else 0) for stride in binary]
    steps = [[(mask, masks[at - 1])] for at, mask in enumerate(masks)]
    steps = [[lambda part, band, m=m: part ^ m[band % 2] for m in step] for step in steps]
    for stride, radix in other:
        steps.append([lambda part, band, d=(stride, radix, by): turn(part, *d) for by in range(1, radix)])
    for step in steps:
        word = value.astype(BF16)
        value = word.astype(F32)
        for move in step:
            pairs = [
                (part * groups + band, move(part, band) * groups + band) for part in range(parts) for band in range(groups)
            ]
            value = value + lax.ppermute(word, ("cells", "bands"), pairs).astype(F32)
    return value


def dot(a, b):
    return jnp.dot(a, b, preferred_element_type=F32)


def dot_t(a, b):
    return lax.dot_general(a, b, (((0,), (0,)), ((), ())), preferred_element_type=F32)


def one_hot(flags):
    return jnp.where(flags, jnp.float32(1), jnp.float32(0)).astype(BF16)


def row_chunks(count):
    return [(first, min(first + 256, count)) for first in range(0, count, 256)]


def tall_dot(rows_of, values):
    return jnp.concatenate([dot(rows_of(first, last), values) for first, last in row_chunks(values.shape[0])], axis=0)


def first_kernel(waves_hbm, cell_hbm, faces_hbm, ham_hbm, start, local, sums, ham, one, columns, waves, cell, faces, rows, sems):
    count = waves.shape[0]
    shared = faces.shape[1]
    padded = one.shape[0] // 2
    chunks = row_chunks(count)
    pairs = [(cell_hbm, cell), (faces_hbm, faces), (waves_hbm, waves)]
    pairs += [(ham_hbm.at[0, first:last], ham.at[first:last]) for first, last in chunks]
    copies = [pltpu.make_async_copy(source, target, sems.at[at]) for at, (source, target) in enumerate(pairs)]
    for copy in copies:
        copy.start()
    rows[...] = jnp.full(rows.shape, -1, F32)
    copies[0].wait()
    copies[1].wait()
    row = cell[...].astype(F32)
    rows[0:1, :count] = row
    rows[1:3, :shared] = faces[...].astype(F32)
    turned_rows = jnp.transpose(rows[...])
    columns[...] = turned_rows
    nodes = lax.broadcasted_iota(jnp.int32, (count, count), 1).astype(F32)
    place = one_hot(turned_rows[:count, 0:1] == nodes)
    pick = one_hot(jnp.concatenate([turned_rows[:padded, 1:2], turned_rows[:padded, 2:3]], axis=0) == row)
    one[...] = pick
    copies[2].wait()
    begin = tall_dot(lambda first, last: place[first:last], waves[...]).astype(BF16)
    start[...] = begin
    for copy in copies[3:]:
        copy.wait()
    local[...] = tall_dot(lambda first, last: ham[first:last], begin)
    sums[...] = dot(pick, local[...].astype(BF16)).astype(BF16)


def middle_kernel(ends, columns, faces, one_t, keep):
    count = one_t.shape[0]
    shared = faces.shape[1]
    padded = one_t.shape[1] // 2
    col = columns[:count, 0:1]
    row = faces[...].astype(F32)
    has_before = jnp.where(ends[0] > 0, jnp.float32(1), jnp.float32(0))
    has_after = jnp.where(ends[1] > 0, jnp.float32(1), jnp.float32(0))
    first = jnp.where(col == row[0:1], jnp.float32(1), jnp.float32(0))
    second = jnp.where(col == row[1:2], jnp.float32(1), jnp.float32(0))
    one_t[...] = jnp.zeros(one_t.shape, BF16)
    one_t[:, :shared] = (first * has_before).astype(BF16)
    one_t[:, padded : padded + shared] = (second * has_after).astype(BF16)
    keep[...] = jnp.broadcast_to(1.0 - jnp.sum(first, axis=1, keepdims=True) * has_before, keep.shape)


def second_kernel(local, before, after, ham, start, one_t, keep, result, block):
    halo = jnp.concatenate([before[...], after[...]], axis=0)
    newer = 0.5 * (local[...] + dot(one_t[...], halo))
    sums = tall_dot(lambda first, last: ham[first:last], newer.astype(BF16))
    result[...] = sums
    block[...] = (sums - start[...].astype(F32) * keep[...]).astype(BF16)


def face_kernel(result, start, one, sums):
    sums[...] = dot(one[...], jnp.concatenate([result[...].astype(BF16), start[...]], axis=1)).astype(BF16)


def third_kernel(result, start, keep, before, after, one_t, *rest):
    blocks, (filtered, gram) = rest[:-2], rest[-2:]
    width = result.shape[1]
    here = jnp.concatenate([before[:, :width], after[:, :width]], axis=0)
    there = jnp.concatenate([before[:, width:], jnp.zeros((after.shape[0], width), BF16)], axis=0)
    halo = dot(one_t[...], jnp.concatenate([here, there], axis=1))
    older = start[...].astype(F32)
    whole = result[...] + halo[:, :width]
    filtered[...] = whole - older
    right = (whole - older * keep[...] - halo[:, width:]).astype(BF16)
    product = dot_t(right, jnp.concatenate([block[...] for block in blocks], axis=1))
    for at in range(len(blocks)):
        gram[at] = jnp.transpose(product[:, at * width : (at + 1) * width]).astype(BF16)


def vmem(count):
    return [pl.BlockSpec(memory_space=pltpu.VMEM)] * count


def body(wavefunctions, hamiltonians, connectivity, face_nodes):
    node_count, width = wavefunctions.shape
    shared = face_nodes.shape[1]
    padded = -(-shared // 32) * 32
    lanes = -(-node_count // 128) * 128
    parts = lax.axis_size("cells")
    groups = lax.axis_size("bands")
    place = lax.axis_index("cells")
    group = lax.axis_index("bands")
    nodal = (node_count, width)
    shape = jax.ShapeDtypeStruct
    params = pltpu.CompilerParams(vmem_limit_bytes=24 * 2**20)

    start, local, sums, ham, one, columns = pl.pallas_call(
        first_kernel,
        out_shape=(
            shape(nodal, BF16),
            shape(nodal, F32),
            shape((2 * padded, width), BF16),
            shape(hamiltonians.shape[1:], BF16),
            shape((2 * padded, node_count), BF16),
            shape((lanes, 8), F32),
        ),
        in_specs=[pl.BlockSpec(memory_space=pltpu.HBM)] * 4,
        out_specs=tuple(vmem(6)),
        scratch_shapes=[
            pltpu.VMEM(nodal, BF16),
            pltpu.VMEM(connectivity.shape, jnp.int32),
            pltpu.VMEM(face_nodes.shape, jnp.int32),
            pltpu.VMEM((8, lanes), F32),
            pltpu.SemaphoreType.DMA((3 + len(row_chunks(node_count)),)),
        ],
        compiler_params=params,
    )(*(pltpu.with_memory_space_constraint(x, pltpu.HBM) for x in (wavefunctions, connectivity, face_nodes, hamiltonians)))

    both = ("cells", "bands")
    chip = digits(groups)[-1] if groups > 1 else (1, 1)

    def pair_swap(first):
        pairs = []
        for part in range(parts):
            other = first + ((part - first) ^ 1)
            for band in range(groups):
                if part >= first and other < parts:
                    pairs.append((part * groups + band, other * groups + band))
                else:
                    pairs.append((part * groups + band, part * groups + turn(band, *chip, 1)))
        return pairs

    odd = place % 2 == 1

    def neighbours(sums):
        low, high = sums[:padded], sums[padded:]
        even_odd = lax.ppermute(jnp.where(odd, low, high), both, pair_swap(0))
        odd_even = lax.ppermute(jnp.where(odd, high, low), both, pair_swap(1))
        return jnp.where(odd, even_odd, odd_even), jnp.where(odd, odd_even, even_odd)

    before, after = neighbours(sums)
    ends = jnp.stack([place, parts - 1 - place]).astype(jnp.int32)
    one_t, keep = pl.pallas_call(
        middle_kernel,
        out_shape=(shape((node_count, 2 * padded), BF16), shape(nodal, F32)),
        in_specs=[pl.BlockSpec(memory_space=pltpu.SMEM)] + vmem(2),
        out_specs=tuple(vmem(2)),
        compiler_params=params,
    )(ends, columns, face_nodes)
    result, block = pl.pallas_call(
        second_kernel,
        out_shape=(shape(nodal, F32), shape(nodal, BF16)),
        in_specs=vmem(7),
        out_specs=tuple(vmem(2)),
        compiler_params=params,
    )(local, before, after, ham, start, one_t, keep)

    blocks = {0: block}
    for stride, radix in reversed(digits(groups)):
        for at in list(blocks):
            for by in range(1, radix):
                blocks[at + by * stride] = lax.ppermute(blocks[at], "bands", turned(groups, stride, radix, radix - by))
    sums = pl.pallas_call(
        face_kernel,
        out_shape=shape((2 * padded, 2 * width), BF16),
        in_specs=vmem(3),
        out_specs=vmem(1)[0],
        compiler_params=params,
    )(result, start, one)
    before, after = neighbours(sums)
    filtered, gram = pl.pallas_call(
        third_kernel,
        out_shape=(shape(nodal, F32), shape((groups, width, width), BF16)),
        in_specs=vmem(6 + groups),
        out_specs=tuple(vmem(2)),
        compiler_params=params,
    )(result, start, keep, before, after, one_t, *(blocks[at] for at in range(groups)))
    total = sum_over_cells(gram) * (1.0 / (parts * node_count))
    radices = digits(groups)
    total = total.reshape(tuple(radix for _, radix in reversed(radices)) + (width, width))
    for at, (stride, radix) in enumerate(radices):
        digit = group // stride % radix
        moved = total
        for by in range(1, radix):
            moved = jnp.where(digit == by, jnp.roll(total, by, axis=len(radices) - 1 - at), moved)
        total = moved
    correlation = total.reshape(groups * width, width)

    place_of = (lax.broadcasted_iota(jnp.int32, (node_count, node_count), 0) == connectivity).astype(BF16)
    top = filtered.astype(BF16)
    rest = filtered - top.astype(F32)
    middle = rest.astype(BF16)
    small = (rest - middle.astype(F32)).astype(BF16)
    return dot(place_of, small) + dot(place_of, middle) + dot(place_of, top), correlation


def solution(mesh):
    placed = (P("cells", "bands"), P("cells", None, None), P("cells", None), P("cells", None))
    return jax.shard_map(
        body,
        mesh=mesh,
        in_specs=placed,
        out_specs=(P("cells", "bands"), P(None, "bands")),
        check_vma=False,
    )
```

```python
import jax
import jax.numpy as jnp
from jax import lax
from jax.experimental import pallas as pl
from jax.experimental.pallas import tpu as pltpu
from jax.sharding import PartitionSpec as P

BF16 = jnp.bfloat16
F32 = jnp.float32


def digits(count):
    stride, left, out = 1, count, []
    for radix in range(2, count + 1):
        while left % radix == 0:
            out.append((stride, radix))
            stride *= radix
            left //= radix
    return out


def turn(index, stride, radix, by):
    digit = index // stride % radix
    return index + ((digit + by) % radix - digit) * stride


def turned(count, stride, radix, by):
    return [(source, turn(source, stride, radix, by)) for source in range(count)]


def sum_over_cells(value):
    parts, groups = lax.axis_size("cells"), lax.axis_size("bands")
    binary = [stride for stride, radix in digits(parts) if radix == 2]
    other = [(stride, radix) for stride, radix in digits(parts) if radix != 2]
    masks = [stride + (stride // 2 if stride > 2 else 0) for stride in binary]
    steps = []
    if len(masks) >= 2:
        first, second = masks[:2]
        steps.append([(first, second), (second, first), (first ^ second, first ^ second)])
        masks = masks[2:]
    steps += [[(mask, mask)] for mask in masks]
    steps = [[lambda part, band, m=m: part ^ m[band % 2] for m in step] for step in steps]
    for stride, radix in other:
        steps.append([lambda part, band, d=(stride, radix, by): turn(part, *d) for by in range(1, radix)])
    for step in steps:
        word = value.astype(BF16)
        words = [word.astype(F32)]
        for move in step:
            pairs = [
                (part * groups + band, move(part, band) * groups + band) for part in range(parts) for band in range(groups)
            ]
            words.append(lax.ppermute(word, ("cells", "bands"), pairs).astype(F32))
        value = words[0] + words[1]
        if len(words) == 4:
            value = value + (words[2] + words[3])
        elif len(words) == 3:
            value = value + words[2]
    return value


def dot(a, b):
    return jnp.dot(a, b, preferred_element_type=F32)


def dot_t(a, b):
    return lax.dot_general(a, b, (((0,), (0,)), ((), ())), preferred_element_type=F32)


def one_hot(flags):
    return jnp.where(flags, jnp.float32(1), jnp.float32(0)).astype(BF16)


def row_chunks(count):
    return [(first, min(first + 256, count)) for first in range(0, count, 256)]


def tall_dot(rows_of, values):
    return jnp.concatenate([dot(rows_of(first, last), values) for first, last in row_chunks(values.shape[0])], axis=0)


def first_kernel(waves_hbm, cell_hbm, faces_hbm, ham_hbm, start, local, sums, ham, one, columns, waves, cell, faces, rows, sems):
    count = waves.shape[0]
    shared = faces.shape[1]
    padded = one.shape[0] // 2
    chunks = row_chunks(count)
    pairs = [(cell_hbm, cell), (faces_hbm, faces), (waves_hbm, waves)]
    pairs += [(ham_hbm.at[0, first:last], ham.at[first:last]) for first, last in chunks]
    copies = [pltpu.make_async_copy(source, target, sems.at[at]) for at, (source, target) in enumerate(pairs)]
    for copy in copies:
        copy.start()
    rows[...] = jnp.full(rows.shape, -1, F32)
    copies[0].wait()
    copies[1].wait()
    row = cell[...].astype(F32)
    rows[0:1, :count] = row
    rows[1:3, :shared] = faces[...].astype(F32)
    turned_rows = jnp.transpose(rows[...])
    columns[...] = turned_rows
    nodes = lax.broadcasted_iota(jnp.int32, (count, count), 1).astype(F32)
    place = one_hot(turned_rows[:count, 0:1] == nodes)
    pick = one_hot(jnp.concatenate([turned_rows[:padded, 1:2], turned_rows[:padded, 2:3]], axis=0) == row)
    one[...] = pick
    copies[2].wait()
    begin = tall_dot(lambda first, last: place[first:last], waves[...]).astype(BF16)
    start[...] = begin
    for copy in copies[3:]:
        copy.wait()
    local[...] = tall_dot(lambda first, last: ham[first:last], begin)
    sums[...] = dot(pick, local[...].astype(BF16)).astype(BF16)


def middle_kernel(ends, columns, faces, one_t, keep):
    count = one_t.shape[0]
    shared = faces.shape[1]
    padded = one_t.shape[1] // 2
    col = columns[:count, 0:1]
    row = faces[...].astype(F32)
    has_before = jnp.where(ends[0] > 0, jnp.float32(1), jnp.float32(0))
    has_after = jnp.where(ends[1] > 0, jnp.float32(1), jnp.float32(0))
    first = jnp.where(col == row[0:1], jnp.float32(1), jnp.float32(0))
    second = jnp.where(col == row[1:2], jnp.float32(1), jnp.float32(0))
    one_t[...] = jnp.zeros(one_t.shape, BF16)
    one_t[:, :shared] = (first * has_before).astype(BF16)
    one_t[:, padded : padded + shared] = (second * has_after).astype(BF16)
    keep[...] = jnp.broadcast_to(1.0 - jnp.sum(first, axis=1, keepdims=True) * has_before, keep.shape)


def second_kernel(local, before, after, ham, start, one_t, keep, result, block):
    halo = jnp.concatenate([before[...], after[...]], axis=0)
    newer = 0.5 * (local[...] + dot(one_t[...], halo))
    sums = tall_dot(lambda first, last: ham[first:last], newer.astype(BF16))
    result[...] = sums
    block[...] = (sums - start[...].astype(F32) * keep[...]).astype(BF16)


def face_kernel(result, start, one, sums):
    sums[...] = dot(one[...], jnp.concatenate([result[...].astype(BF16), start[...]], axis=1)).astype(BF16)


def third_kernel(result, start, keep, before, after, one_t, *rest):
    blocks, (filtered, gram) = rest[:-2], rest[-2:]
    width = result.shape[1]
    here = jnp.concatenate([before[:, :width], after[:, :width]], axis=0)
    there = jnp.concatenate([before[:, width:], jnp.zeros((after.shape[0], width), BF16)], axis=0)
    halo = dot(one_t[...], jnp.concatenate([here, there], axis=1))
    older = start[...].astype(F32)
    whole = result[...] + halo[:, :width]
    filtered[...] = whole - older
    right = (whole - older * keep[...] - halo[:, width:]).astype(BF16)
    product = dot_t(right, jnp.concatenate([block[...] for block in blocks], axis=1))
    for at in range(len(blocks)):
        gram[at] = jnp.transpose(product[:, at * width : (at + 1) * width]).astype(BF16)


def vmem(count):
    return [pl.BlockSpec(memory_space=pltpu.VMEM)] * count


def body(wavefunctions, hamiltonians, connectivity, face_nodes):
    node_count, width = wavefunctions.shape
    shared = face_nodes.shape[1]
    padded = -(-shared // 32) * 32
    lanes = -(-node_count // 128) * 128
    parts = lax.axis_size("cells")
    groups = lax.axis_size("bands")
    place = lax.axis_index("cells")
    group = lax.axis_index("bands")
    nodal = (node_count, width)
    shape = jax.ShapeDtypeStruct
    params = pltpu.CompilerParams(vmem_limit_bytes=24 * 2**20)

    start, local, sums, ham, one, columns = pl.pallas_call(
        first_kernel,
        out_shape=(
            shape(nodal, BF16),
            shape(nodal, F32),
            shape((2 * padded, width), BF16),
            shape(hamiltonians.shape[1:], BF16),
            shape((2 * padded, node_count), BF16),
            shape((lanes, 8), F32),
        ),
        in_specs=[pl.BlockSpec(memory_space=pltpu.HBM)] * 4,
        out_specs=tuple(vmem(6)),
        scratch_shapes=[
            pltpu.VMEM(nodal, BF16),
            pltpu.VMEM(connectivity.shape, jnp.int32),
            pltpu.VMEM(face_nodes.shape, jnp.int32),
            pltpu.VMEM((8, lanes), F32),
            pltpu.SemaphoreType.DMA((3 + len(row_chunks(node_count)),)),
        ],
        compiler_params=params,
    )(*(pltpu.with_memory_space_constraint(x, pltpu.HBM) for x in (wavefunctions, connectivity, face_nodes, hamiltonians)))

    both = ("cells", "bands")
    chip = digits(groups)[-1] if groups > 1 else (1, 1)

    def pair_swap(first):
        pairs = []
        for part in range(parts):
            other = first + ((part - first) ^ 1)
            for band in range(groups):
                if part >= first and other < parts:
                    pairs.append((part * groups + band, other * groups + band))
                else:
                    pairs.append((part * groups + band, part * groups + turn(band, *chip, 1)))
        return pairs

    odd = place % 2 == 1
    even = place % 2 == 0

    def neighbours(sums):
        low, high = sums[:padded], sums[padded:]
        even_odd = lax.ppermute(jnp.where(odd, low, high), both, pair_swap(0))
        odd_even = lax.ppermute(jnp.where(odd, high, low), both, pair_swap(1))
        return jnp.where(even, odd_even, even_odd), jnp.where(even, even_odd, odd_even)

    before, after = neighbours(sums)
    ends = jnp.stack([place, parts - 1 - place]).astype(jnp.int32)
    one_t, keep = pl.pallas_call(
        middle_kernel,
        out_shape=(shape((node_count, 2 * padded), BF16), shape(nodal, F32)),
        in_specs=[pl.BlockSpec(memory_space=pltpu.SMEM)] + vmem(2),
        out_specs=tuple(vmem(2)),
        compiler_params=params,
    )(ends, columns, face_nodes)
    result, block = pl.pallas_call(
        second_kernel,
        out_shape=(shape(nodal, F32), shape(nodal, BF16)),
        in_specs=vmem(7),
        out_specs=tuple(vmem(2)),
        compiler_params=params,
    )(local, before, after, ham, start, one_t, keep)

    blocks = {0: block}
    for stride, radix in reversed(digits(groups)):
        for at in list(blocks):
            for by in range(1, radix):
                blocks[at + by * stride] = lax.ppermute(blocks[at], "bands", turned(groups, stride, radix, radix - by))
    sums = pl.pallas_call(
        face_kernel,
        out_shape=shape((2 * padded, 2 * width), BF16),
        in_specs=vmem(3),
        out_specs=vmem(1)[0],
        compiler_params=params,
    )(result, start, one)
    before, after = neighbours(sums)
    filtered, gram = pl.pallas_call(
        third_kernel,
        out_shape=(shape(nodal, F32), shape((groups, width, width), BF16)),
        in_specs=vmem(6 + groups),
        out_specs=tuple(vmem(2)),
        compiler_params=params,
    )(result, start, keep, before, after, one_t, *(blocks[at] for at in range(groups)))
    total = sum_over_cells(gram) * (1.0 / (parts * node_count))
    radices = digits(groups)
    total = total.reshape(tuple(radix for _, radix in reversed(radices)) + (width, width))
    for at, (stride, radix) in enumerate(radices):
        digit = group // stride % radix
        moved = total
        for by in range(1, radix):
            moved = jnp.where(digit == by, jnp.roll(total, by, axis=len(radices) - 1 - at), moved)
        total = moved
    correlation = total.reshape(groups * width, width)

    place_of = (lax.broadcasted_iota(jnp.int32, (node_count, node_count), 0) == connectivity).astype(BF16)
    top = filtered.astype(BF16)
    rest = filtered - top.astype(F32)
    middle = rest.astype(BF16)
    small = (rest - middle.astype(F32)).astype(BF16)
    return dot(place_of, small) + dot(place_of, middle) + dot(place_of, top), correlation


def solution(mesh):
    placed = (P("cells", "bands"), P("cells", None, None), P("cells", None), P("cells", None))
    return jax.shard_map(
        body,
        mesh=mesh,
        in_specs=placed,
        out_specs=(P("cells", "bands"), P(None, "bands")),
        check_vma=False,
    )
```

```python
import jax
import jax.numpy as jnp
from jax import lax
from jax.experimental import pallas as pl
from jax.experimental.pallas import tpu as pltpu
from jax.sharding import PartitionSpec as P

BF16 = jnp.bfloat16
F32 = jnp.float32


def digits(count):
    stride, left, out = 1, count, []
    for radix in range(2, count + 1):
        while left % radix == 0:
            out.append((stride, radix))
            stride *= radix
            left //= radix
    return out


def turn(index, stride, radix, by):
    digit = index // stride % radix
    return index + ((digit + by) % radix - digit) * stride


def turned(count, stride, radix, by):
    return [(source, turn(source, stride, radix, by)) for source in range(count)]


def sum_over_cells(value):
    parts, groups = lax.axis_size("cells"), lax.axis_size("bands")
    binary = [stride for stride, radix in digits(parts) if radix == 2]
    other = [(stride, radix) for stride, radix in digits(parts) if radix != 2]
    masks = [stride + (stride // 2 if stride > 2 else 0) for stride in binary]
    steps = []
    if len(masks) >= 2:
        first, second = masks[:2]
        steps.append([(first, second), (second, first), (first ^ second, first ^ second)])
        masks = masks[2:]
    steps += [[(mask, mask)] for mask in masks]
    steps = [[lambda part, band, m=m: part ^ m[band % 2] for m in step] for step in steps]
    for stride, radix in other:
        steps.append([lambda part, band, d=(stride, radix, by): turn(part, *d) for by in range(1, radix)])
    for step in steps:
        word = value.astype(BF16)
        words = [word.astype(F32)]
        for move in step:
            pairs = [
                (part * groups + band, move(part, band) * groups + band) for part in range(parts) for band in range(groups)
            ]
            words.append(lax.ppermute(word, ("cells", "bands"), pairs).astype(F32))
        value = words[0] + words[1]
        if len(words) == 4:
            value = value + (words[2] + words[3])
        elif len(words) == 3:
            value = value + words[2]
    return value


def dot(a, b):
    return jnp.dot(a, b, preferred_element_type=F32)


def dot_t(a, b):
    return lax.dot_general(a, b, (((0,), (0,)), ((), ())), preferred_element_type=F32)


def one_hot(flags):
    return jnp.where(flags, jnp.float32(1), jnp.float32(0)).astype(BF16)


def row_chunks(count):
    return [(first, min(first + 256, count)) for first in range(0, count, 256)]


def tall_dot(rows_of, values):
    return jnp.concatenate([dot(rows_of(first, last), values) for first, last in row_chunks(values.shape[0])], axis=0)


def first_kernel(waves_hbm, cell_hbm, faces_hbm, ham_hbm, start, local, sums, ham, one, columns, waves, cell, faces, rows, sems):
    count = waves.shape[0]
    shared = faces.shape[1]
    padded = one.shape[0] // 2
    chunks = row_chunks(count)
    pairs = [(cell_hbm, cell), (faces_hbm, faces), (waves_hbm, waves)]
    pairs += [(ham_hbm.at[0, first:last], ham.at[first:last]) for first, last in chunks]
    copies = [pltpu.make_async_copy(source, target, sems.at[at]) for at, (source, target) in enumerate(pairs)]
    for copy in copies:
        copy.start()
    rows[...] = jnp.full(rows.shape, -1, F32)
    copies[0].wait()
    copies[1].wait()
    row = cell[...].astype(F32)
    rows[0:1, :count] = row
    rows[1:3, :shared] = faces[...].astype(F32)
    turned_rows = jnp.transpose(rows[...])
    columns[...] = turned_rows
    nodes = lax.broadcasted_iota(jnp.int32, (count, count), 1).astype(F32)
    place = one_hot(turned_rows[:count, 0:1] == nodes)
    pick = one_hot(jnp.concatenate([turned_rows[:padded, 1:2], turned_rows[:padded, 2:3]], axis=0) == row)
    one[...] = pick
    copies[2].wait()
    begin = tall_dot(lambda first, last: place[first:last], waves[...]).astype(BF16)
    start[...] = begin
    for copy in copies[3:]:
        copy.wait()
    local[...] = tall_dot(lambda first, last: ham[first:last], begin)
    sums[...] = dot(pick, local[...].astype(BF16)).astype(BF16)


def middle_kernel(ends, columns, faces, local, ham, one_t, keep, mine, border):
    count = one_t.shape[0]
    shared = faces.shape[1]
    padded = one_t.shape[1] // 2
    col = columns[:count, 0:1]
    row = faces[...].astype(F32)
    has_before = jnp.where(ends[0] > 0, jnp.float32(1), jnp.float32(0))
    has_after = jnp.where(ends[1] > 0, jnp.float32(1), jnp.float32(0))
    first = jnp.where(col == row[0:1], jnp.float32(1), jnp.float32(0))
    second = jnp.where(col == row[1:2], jnp.float32(1), jnp.float32(0))
    one_t[...] = jnp.zeros(one_t.shape, BF16)
    one_t[:, :shared] = (first * has_before).astype(BF16)
    one_t[:, padded : padded + shared] = (second * has_after).astype(BF16)
    keep[...] = jnp.broadcast_to(1.0 - jnp.sum(first, axis=1, keepdims=True) * has_before, keep.shape)
    half = (0.5 * local[...]).astype(BF16)
    both = tall_dot(lambda first, last: ham[first:last], jnp.concatenate([half, one_t[...]], axis=1))
    width = local.shape[1]
    mine[...] = both[:, :width]
    border[...] = both[:, width:].astype(BF16)


def second_kernel(before, after, mine, border, start, keep, result, block):
    halo = 0.5 * jnp.concatenate([before[...], after[...]], axis=0).astype(F32)
    sums = mine[...] + dot(border[...], halo.astype(BF16))
    result[...] = sums
    block[...] = (sums - start[...].astype(F32) * keep[...]).astype(BF16)


def face_kernel(result, start, one, sums):
    sums[...] = dot(one[...], jnp.concatenate([result[...].astype(BF16), start[...]], axis=1)).astype(BF16)


def third_kernel(result, start, keep, before, after, one_t, *rest):
    blocks, (filtered, gram) = rest[:-2], rest[-2:]
    width = result.shape[1]
    here = jnp.concatenate([before[:, :width], after[:, :width]], axis=0)
    there = jnp.concatenate([before[:, width:], jnp.zeros((after.shape[0], width), BF16)], axis=0)
    halo = dot(one_t[...], jnp.concatenate([here, there], axis=1))
    older = start[...].astype(F32)
    whole = result[...] + halo[:, :width]
    filtered[...] = whole - older
    right = (whole - older * keep[...] - halo[:, width:]).astype(BF16)
    product = dot_t(right, jnp.concatenate([block[...] for block in blocks], axis=1))
    for at in range(len(blocks)):
        gram[at] = jnp.transpose(product[:, at * width : (at + 1) * width]).astype(BF16)


def vmem(count):
    return [pl.BlockSpec(memory_space=pltpu.VMEM)] * count


def body(wavefunctions, hamiltonians, connectivity, face_nodes):
    node_count, width = wavefunctions.shape
    shared = face_nodes.shape[1]
    padded = -(-shared // 32) * 32
    lanes = -(-node_count // 128) * 128
    parts = lax.axis_size("cells")
    groups = lax.axis_size("bands")
    place = lax.axis_index("cells")
    group = lax.axis_index("bands")
    nodal = (node_count, width)
    shape = jax.ShapeDtypeStruct
    params = pltpu.CompilerParams(vmem_limit_bytes=24 * 2**20)

    start, local, sums, ham, one, columns = pl.pallas_call(
        first_kernel,
        out_shape=(
            shape(nodal, BF16),
            shape(nodal, F32),
            shape((2 * padded, width), BF16),
            shape(hamiltonians.shape[1:], BF16),
            shape((2 * padded, node_count), BF16),
            shape((lanes, 8), F32),
        ),
        in_specs=[pl.BlockSpec(memory_space=pltpu.HBM)] * 4,
        out_specs=tuple(vmem(6)),
        scratch_shapes=[
            pltpu.VMEM(nodal, BF16),
            pltpu.VMEM(connectivity.shape, jnp.int32),
            pltpu.VMEM(face_nodes.shape, jnp.int32),
            pltpu.VMEM((8, lanes), F32),
            pltpu.SemaphoreType.DMA((3 + len(row_chunks(node_count)),)),
        ],
        compiler_params=params,
    )(*(pltpu.with_memory_space_constraint(x, pltpu.HBM) for x in (wavefunctions, connectivity, face_nodes, hamiltonians)))

    both = ("cells", "bands")
    chip = digits(groups)[-1] if groups > 1 else (1, 1)

    def pair_swap(first):
        pairs = []
        for part in range(parts):
            other = first + ((part - first) ^ 1)
            for band in range(groups):
                if part >= first and other < parts:
                    pairs.append((part * groups + band, other * groups + band))
                else:
                    pairs.append((part * groups + band, part * groups + turn(band, *chip, 1)))
        return pairs

    odd = place % 2 == 1
    even = place % 2 == 0

    def neighbours(sums):
        low, high = sums[:padded], sums[padded:]
        even_odd = lax.ppermute(jnp.where(odd, low, high), both, pair_swap(0))
        odd_even = lax.ppermute(jnp.where(odd, high, low), both, pair_swap(1))
        return jnp.where(even, odd_even, even_odd), jnp.where(even, even_odd, odd_even)

    before, after = neighbours(sums)
    ends = jnp.stack([place, parts - 1 - place]).astype(jnp.int32)
    one_t, keep, mine, border = pl.pallas_call(
        middle_kernel,
        out_shape=(
            shape((node_count, 2 * padded), BF16),
            shape(nodal, F32),
            shape(nodal, F32),
            shape((node_count, 2 * padded), BF16),
        ),
        in_specs=[pl.BlockSpec(memory_space=pltpu.SMEM)] + vmem(4),
        out_specs=tuple(vmem(4)),
        compiler_params=params,
    )(ends, columns, face_nodes, local, ham)
    result, block = pl.pallas_call(
        second_kernel,
        out_shape=(shape(nodal, F32), shape(nodal, BF16)),
        in_specs=vmem(6),
        out_specs=tuple(vmem(2)),
        compiler_params=params,
    )(before, after, mine, border, start, keep)

    blocks = {0: block}
    for stride, radix in reversed(digits(groups)):
        for at in list(blocks):
            for by in range(1, radix):
                blocks[at + by * stride] = lax.ppermute(blocks[at], "bands", turned(groups, stride, radix, radix - by))
    sums = pl.pallas_call(
        face_kernel,
        out_shape=shape((2 * padded, 2 * width), BF16),
        in_specs=vmem(3),
        out_specs=vmem(1)[0],
        compiler_params=params,
    )(result, start, one)
    before, after = neighbours(sums)
    filtered, gram = pl.pallas_call(
        third_kernel,
        out_shape=(shape(nodal, F32), shape((groups, width, width), BF16)),
        in_specs=vmem(6 + groups),
        out_specs=tuple(vmem(2)),
        compiler_params=params,
    )(result, start, keep, before, after, one_t, *(blocks[at] for at in range(groups)))
    total = sum_over_cells(gram) * (1.0 / (parts * node_count))
    radices = digits(groups)
    total = total.reshape(tuple(radix for _, radix in reversed(radices)) + (width, width))
    for at, (stride, radix) in enumerate(radices):
        digit = group // stride % radix
        moved = total
        for by in range(1, radix):
            moved = jnp.where(digit == by, jnp.roll(total, by, axis=len(radices) - 1 - at), moved)
        total = moved
    correlation = total.reshape(groups * width, width)

    place_of = (lax.broadcasted_iota(jnp.int32, (node_count, node_count), 0) == connectivity).astype(BF16)
    top = filtered.astype(BF16)
    rest = filtered - top.astype(F32)
    middle = rest.astype(BF16)
    small = (rest - middle.astype(F32)).astype(BF16)
    return dot(place_of, small) + dot(place_of, middle) + dot(place_of, top), correlation


def solution(mesh):
    placed = (P("cells", "bands"), P("cells", None, None), P("cells", None), P("cells", None))
    return jax.shard_map(
        body,
        mesh=mesh,
        in_specs=placed,
        out_specs=(P("cells", "bands"), P(None, "bands")),
        check_vma=False,
    )
```

```python
import jax
import jax.numpy as jnp
from jax import lax
from jax.experimental import pallas as pl
from jax.experimental.pallas import tpu as pltpu
from jax.sharding import PartitionSpec as P

BF16 = jnp.bfloat16
F32 = jnp.float32


def digits(count):
    stride, left, out = 1, count, []
    for radix in range(2, count + 1):
        while left % radix == 0:
            out.append((stride, radix))
            stride *= radix
            left //= radix
    return out


def turn(index, stride, radix, by):
    digit = index // stride % radix
    return index + ((digit + by) % radix - digit) * stride


def turned(count, stride, radix, by):
    return [(source, turn(source, stride, radix, by)) for source in range(count)]


def sum_over_cells(value):
    parts, groups = lax.axis_size("cells"), lax.axis_size("bands")
    binary = [stride for stride, radix in digits(parts) if radix == 2]
    other = [(stride, radix) for stride, radix in digits(parts) if radix != 2]
    masks = [stride + (stride // 2 if stride > 2 else 0) for stride in binary]
    steps = []
    if len(masks) >= 2:
        first, second = masks[:2]
        steps.append([(first, second), (second, first), (first ^ second, first ^ second)])
        masks = masks[2:]
    steps += [[(mask, mask)] for mask in masks]
    steps = [[lambda part, band, m=m: part ^ m[band % 2] for m in step] for step in steps]
    for stride, radix in other:
        steps.append([lambda part, band, d=(stride, radix, by): turn(part, *d) for by in range(1, radix)])
    for step in steps:
        word = value.astype(BF16)
        words = [word.astype(F32)]
        for move in step:
            pairs = [
                (part * groups + band, move(part, band) * groups + band) for part in range(parts) for band in range(groups)
            ]
            words.append(lax.ppermute(word, ("cells", "bands"), pairs).astype(F32))
        value = words[0] + words[1]
        if len(words) == 4:
            value = value + (words[2] + words[3])
        elif len(words) == 3:
            value = value + words[2]
    return value


def dot(a, b):
    return jnp.dot(a, b, preferred_element_type=F32)


def dot_t(a, b):
    return lax.dot_general(a, b, (((0,), (0,)), ((), ())), preferred_element_type=F32)


def one_hot(flags):
    return jnp.where(flags, jnp.float32(1), jnp.float32(0)).astype(BF16)


def row_chunks(count):
    return [(first, min(first + 256, count)) for first in range(0, count, 256)]


def tall_dot(rows_of, values):
    return jnp.concatenate([dot(rows_of(first, last), values) for first, last in row_chunks(values.shape[0])], axis=0)


def first_kernel(waves_hbm, cell_hbm, faces_hbm, ham_hbm, start, local, sums, ham, one, columns, waves, cell, faces, rows, sems):
    count = waves.shape[0]
    shared = faces.shape[1]
    padded = one.shape[0] // 2
    chunks = row_chunks(count)
    pairs = [(cell_hbm, cell), (faces_hbm, faces), (waves_hbm, waves)]
    pairs += [(ham_hbm.at[0, first:last], ham.at[first:last]) for first, last in chunks]
    copies = [pltpu.make_async_copy(source, target, sems.at[at]) for at, (source, target) in enumerate(pairs)]
    for copy in copies:
        copy.start()
    rows[...] = jnp.full(rows.shape, -1, F32)
    copies[0].wait()
    copies[1].wait()
    row = cell[...].astype(F32)
    rows[0:1, :count] = row
    rows[1:3, :shared] = faces[...].astype(F32)
    turned_rows = jnp.transpose(rows[...])
    columns[...] = turned_rows
    nodes = lax.broadcasted_iota(jnp.int32, (count, count), 1).astype(F32)
    place = one_hot(turned_rows[:count, 0:1] == nodes)
    pick = one_hot(jnp.concatenate([turned_rows[:padded, 1:2], turned_rows[:padded, 2:3]], axis=0) == row)
    one[...] = pick
    copies[2].wait()
    begin = tall_dot(lambda first, last: place[first:last], waves[...]).astype(BF16)
    start[...] = begin
    for copy in copies[3:]:
        copy.wait()
    local[...] = tall_dot(lambda first, last: ham[first:last], begin)
    sums[...] = dot(pick, local[...].astype(BF16)).astype(BF16)


def middle_kernel(columns, faces, local, ham, one_t, keep, mine, border):
    count = one_t.shape[0]
    shared = faces.shape[1]
    padded = one_t.shape[1] // 2
    col = columns[:count, 0:1]
    row = faces[...].astype(F32)
    part, parts = lax.axis_index("cells"), lax.axis_size("cells")
    has_before = jnp.where(part > 0, jnp.float32(1), jnp.float32(0))
    has_after = jnp.where(part < parts - 1, jnp.float32(1), jnp.float32(0))
    first = jnp.where(col == row[0:1], jnp.float32(1), jnp.float32(0))
    second = jnp.where(col == row[1:2], jnp.float32(1), jnp.float32(0))
    one_t[...] = jnp.zeros(one_t.shape, BF16)
    one_t[:, :shared] = (first * has_before).astype(BF16)
    one_t[:, padded : padded + shared] = (second * has_after).astype(BF16)
    keep[...] = jnp.broadcast_to(1.0 - jnp.sum(first, axis=1, keepdims=True) * has_before, keep.shape)
    half = (0.5 * local[...]).astype(BF16)
    both = tall_dot(lambda first, last: ham[first:last], jnp.concatenate([half, one_t[...]], axis=1))
    width = local.shape[1]
    mine[...] = both[:, :width]
    border[...] = both[:, width:].astype(BF16)


def second_kernel(before, after, mine, border, start, keep, result, block):
    halo = 0.5 * jnp.concatenate([before[...], after[...]], axis=0).astype(F32)
    sums = mine[...] + dot(border[...], halo.astype(BF16))
    result[...] = sums
    block[...] = (sums - start[...].astype(F32) * keep[...]).astype(BF16)


def face_kernel(result, start, one, sums):
    sums[...] = dot(one[...], jnp.concatenate([result[...].astype(BF16), start[...]], axis=1)).astype(BF16)


def third_kernel(result, start, keep, before, after, one_t, *rest):
    blocks, (filtered, gram) = rest[:-2], rest[-2:]
    width = result.shape[1]
    here = jnp.concatenate([before[:, :width], after[:, :width]], axis=0)
    there = jnp.concatenate([before[:, width:], jnp.zeros((after.shape[0], width), BF16)], axis=0)
    halo = dot(one_t[...], jnp.concatenate([here, there], axis=1))
    older = start[...].astype(F32)
    whole = result[...] + halo[:, :width]
    filtered[...] = whole - older
    right = (whole - older * keep[...] - halo[:, width:]).astype(BF16)
    product = dot_t(right, jnp.concatenate([block[...] for block in blocks], axis=1))
    group = lax.axis_index("bands")
    for at in range(len(blocks)):
        target = 0
        for stride, radix in digits(len(blocks)):
            target = target + (group // stride + at // stride) % radix * stride
        gram[target] = jnp.transpose(product[:, at * width : (at + 1) * width]).astype(BF16)


def vmem(count):
    return [pl.BlockSpec(memory_space=pltpu.VMEM)] * count


def body(wavefunctions, hamiltonians, connectivity, face_nodes):
    node_count, width = wavefunctions.shape
    shared = face_nodes.shape[1]
    padded = -(-shared // 32) * 32
    lanes = -(-node_count // 128) * 128
    parts = lax.axis_size("cells")
    groups = lax.axis_size("bands")
    place = lax.axis_index("cells")
    nodal = (node_count, width)
    shape = jax.ShapeDtypeStruct
    params = pltpu.CompilerParams(vmem_limit_bytes=24 * 2**20)

    start, local, sums, ham, one, columns = pl.pallas_call(
        first_kernel,
        out_shape=(
            shape(nodal, BF16),
            shape(nodal, F32),
            shape((2 * padded, width), BF16),
            shape(hamiltonians.shape[1:], BF16),
            shape((2 * padded, node_count), BF16),
            shape((lanes, 8), F32),
        ),
        in_specs=[pl.BlockSpec(memory_space=pltpu.HBM)] * 4,
        out_specs=tuple(vmem(6)),
        scratch_shapes=[
            pltpu.VMEM(nodal, BF16),
            pltpu.VMEM(connectivity.shape, jnp.int32),
            pltpu.VMEM(face_nodes.shape, jnp.int32),
            pltpu.VMEM((8, lanes), F32),
            pltpu.SemaphoreType.DMA((3 + len(row_chunks(node_count)),)),
        ],
        compiler_params=params,
    )(*(pltpu.with_memory_space_constraint(x, pltpu.HBM) for x in (wavefunctions, connectivity, face_nodes, hamiltonians)))

    both = ("cells", "bands")
    chip = digits(groups)[-1] if groups > 1 else (1, 1)

    def pair_swap(first):
        pairs = []
        for part in range(parts):
            other = first + ((part - first) ^ 1)
            for band in range(groups):
                if part >= first and other < parts:
                    pairs.append((part * groups + band, other * groups + band))
                else:
                    pairs.append((part * groups + band, part * groups + turn(band, *chip, 1)))
        return pairs

    odd = place % 2 == 1
    even = place % 2 == 0

    def neighbours(sums):
        low, high = sums[:padded], sums[padded:]
        even_odd = lax.ppermute(jnp.where(odd, low, high), both, pair_swap(0))
        odd_even = lax.ppermute(jnp.where(odd, high, low), both, pair_swap(1))
        return jnp.where(even, odd_even, even_odd), jnp.where(even, even_odd, odd_even)

    before, after = neighbours(sums)
    one_t, keep, mine, border = pl.pallas_call(
        middle_kernel,
        out_shape=(
            shape((node_count, 2 * padded), BF16),
            shape(nodal, F32),
            shape(nodal, F32),
            shape((node_count, 2 * padded), BF16),
        ),
        in_specs=vmem(4),
        out_specs=tuple(vmem(4)),
        compiler_params=params,
    )(columns, face_nodes, local, ham)
    result, block = pl.pallas_call(
        second_kernel,
        out_shape=(shape(nodal, F32), shape(nodal, BF16)),
        in_specs=vmem(6),
        out_specs=tuple(vmem(2)),
        compiler_params=params,
    )(before, after, mine, border, start, keep)

    blocks = {0: block}
    for stride, radix in reversed(digits(groups)):
        for at in list(blocks):
            for by in range(1, radix):
                blocks[at + by * stride] = lax.ppermute(blocks[at], "bands", turned(groups, stride, radix, radix - by))
    sums = pl.pallas_call(
        face_kernel,
        out_shape=shape((2 * padded, 2 * width), BF16),
        in_specs=vmem(3),
        out_specs=vmem(1)[0],
        compiler_params=params,
    )(result, start, one)
    before, after = neighbours(sums)
    filtered, gram = pl.pallas_call(
        third_kernel,
        out_shape=(shape(nodal, F32), shape((groups, width, width), BF16)),
        in_specs=vmem(6 + groups),
        out_specs=tuple(vmem(2)),
        compiler_params=params,
    )(result, start, keep, before, after, one_t, *(blocks[at] for at in range(groups)))
    total = sum_over_cells(gram) * (1.0 / (parts * node_count))
    correlation = total.reshape(groups * width, width)

    place_of = (lax.broadcasted_iota(jnp.int32, (node_count, node_count), 0) == connectivity).astype(BF16)
    top = filtered.astype(BF16)
    rest = filtered - top.astype(F32)
    middle = rest.astype(BF16)
    small = (rest - middle.astype(F32)).astype(BF16)
    return dot(place_of, small) + dot(place_of, middle) + dot(place_of, top), correlation


def solution(mesh):
    placed = (P("cells", "bands"), P("cells", None, None), P("cells", None), P("cells", None))
    return jax.shard_map(
        body,
        mesh=mesh,
        in_specs=placed,
        out_specs=(P("cells", "bands"), P(None, "bands")),
        check_vma=False,
    )
```

```python
import jax
import jax.numpy as jnp
from jax import lax
from jax.experimental import pallas as pl
from jax.experimental.pallas import tpu as pltpu
from jax.sharding import PartitionSpec as P

BF16 = jnp.bfloat16
F32 = jnp.float32


def digits(count):
    stride, left, out = 1, count, []
    for radix in range(2, count + 1):
        while left % radix == 0:
            out.append((stride, radix))
            stride *= radix
            left //= radix
    return out


def turn(index, stride, radix, by):
    digit = index // stride % radix
    return index + ((digit + by) % radix - digit) * stride


def turned(count, stride, radix, by):
    return [(source, turn(source, stride, radix, by)) for source in range(count)]


def sum_over_cells(value):
    parts, groups = lax.axis_size("cells"), lax.axis_size("bands")
    binary = [stride for stride, radix in digits(parts) if radix == 2]
    other = [(stride, radix) for stride, radix in digits(parts) if radix != 2]
    masks = [stride + (stride // 2 if stride > 2 else 0) for stride in binary]
    steps = []
    if len(masks) >= 2:
        first, second = masks[:2]
        steps.append([(first, second), (second, first), (first ^ second, first ^ second)])
        masks = masks[2:]
    steps += [[(mask, mask)] for mask in masks]
    steps = [[lambda part, band, m=m: part ^ m[band % 2] for m in step] for step in steps]
    for stride, radix in other:
        steps.append([lambda part, band, d=(stride, radix, by): turn(part, *d) for by in range(1, radix)])
    kind = BF16 if len(steps) <= 3 else F32
    for step in steps:
        word = value.astype(kind)
        words = [word.astype(F32)]
        for move in step:
            pairs = [
                (part * groups + band, move(part, band) * groups + band) for part in range(parts) for band in range(groups)
            ]
            words.append(lax.ppermute(word, ("cells", "bands"), pairs).astype(F32))
        value = words[0] + words[1]
        if len(words) == 4:
            value = value + (words[2] + words[3])
        elif len(words) == 3:
            value = value + words[2]
    return value


def dot(a, b):
    return jnp.dot(a, b, preferred_element_type=F32)


def dot_t(a, b):
    return lax.dot_general(a, b, (((0,), (0,)), ((), ())), preferred_element_type=F32)


def one_hot(flags):
    return jnp.where(flags, jnp.float32(1), jnp.float32(0)).astype(BF16)


def row_chunks(count):
    return [(first, min(first + 368, count)) for first in range(0, count, 368)]


def tall_dot(rows_of, values, count=None):
    chunks = row_chunks(count or values.shape[0])
    return jnp.concatenate([dot(rows_of(first, last), values) for first, last in chunks], axis=0)


def first_kernel(waves_hbm, cell_hbm, faces_hbm, ham_hbm, start, local, sums, ham, one, columns, waves, cell, faces, rows, sems):
    count = waves.shape[0]
    shared = faces.shape[1]
    padded = one.shape[0] // 2
    chunks = row_chunks(count)
    pairs = [(cell_hbm, cell), (faces_hbm, faces), (waves_hbm, waves)]
    pairs += [(ham_hbm.at[0, first:last], ham.at[first:last]) for first, last in chunks]
    copies = [pltpu.make_async_copy(source, target, sems.at[at]) for at, (source, target) in enumerate(pairs)]
    for copy in copies:
        copy.start()
    rows[...] = jnp.full(rows.shape, -1, F32)
    copies[0].wait()
    copies[1].wait()
    row = cell[...].astype(F32)
    rows[0:1, :count] = row
    rows[1:3, :shared] = faces[...].astype(F32)
    turned_rows = jnp.transpose(rows[...])
    columns[...] = turned_rows
    nodes = lax.broadcasted_iota(jnp.int32, (count, count), 1).astype(F32)
    place = one_hot(turned_rows[:count, 0:1] == nodes)
    pick = one_hot(jnp.concatenate([turned_rows[:padded, 1:2], turned_rows[:padded, 2:3]], axis=0) == row)
    one[...] = pick
    copies[2].wait()
    begin = tall_dot(lambda first, last: place[first:last], waves[...]).astype(BF16)
    start[...] = begin
    for copy in copies[3:]:
        copy.wait()
    local[...] = tall_dot(lambda first, last: ham[first:last], begin)
    sums[...] = dot(pick, local[...].astype(BF16)).astype(BF16)


def middle_kernel(columns, faces, local, ham, one_t, keep, mine, border):
    count = one_t.shape[0]
    shared = faces.shape[1]
    padded = one_t.shape[1] // 2
    col = columns[:count, 0:1]
    row = faces[...].astype(F32)
    part, parts = lax.axis_index("cells"), lax.axis_size("cells")
    has_before = jnp.where(part > 0, jnp.float32(1), jnp.float32(0))
    has_after = jnp.where(part < parts - 1, jnp.float32(1), jnp.float32(0))
    first = jnp.where(col == row[0:1], jnp.float32(1), jnp.float32(0))
    second = jnp.where(col == row[1:2], jnp.float32(1), jnp.float32(0))
    one_t[...] = jnp.zeros(one_t.shape, BF16)
    one_t[:, :shared] = (first * has_before).astype(BF16)
    one_t[:, padded : padded + shared] = (second * has_after).astype(BF16)
    keep[...] = jnp.broadcast_to(1.0 - jnp.sum(first, axis=1, keepdims=True) * has_before, keep.shape)
    half = (0.5 * local[...]).astype(BF16)
    both = tall_dot(lambda first, last: ham[first:last], jnp.concatenate([half, one_t[...]], axis=1))
    width = local.shape[1]
    mine[...] = both[:, :width]
    border[...] = both[:, width:].astype(BF16)


def second_kernel(before, after, mine, border, start, keep, result, block):
    halo = 0.5 * jnp.concatenate([before[...], after[...]], axis=0).astype(F32)
    sums = mine[...] + tall_dot(lambda first, last: border[first:last], halo.astype(BF16), border.shape[0])
    result[...] = sums
    block[...] = (sums - start[...].astype(F32) * keep[...]).astype(BF16)


def face_kernel(result, start, one, sums):
    sums[...] = dot(one[...], jnp.concatenate([result[...].astype(BF16), start[...]], axis=1)).astype(BF16)


def third_kernel(result, start, keep, before, after, one_t, *rest):
    blocks, (filtered, gram) = rest[:-2], rest[-2:]
    width = result.shape[1]
    here = jnp.concatenate([before[:, :width], after[:, :width]], axis=0)
    there = jnp.concatenate([before[:, width:], jnp.zeros((after.shape[0], width), BF16)], axis=0)
    halo_in = jnp.concatenate([here, there], axis=1)
    halo = tall_dot(lambda first, last: one_t[first:last], halo_in, one_t.shape[0])
    older = start[...].astype(F32)
    whole = result[...] + halo[:, :width]
    filtered[...] = whole - older
    right = (whole - older * keep[...] - halo[:, width:]).astype(BF16)
    product = dot_t(right, jnp.concatenate([block[...] for block in blocks], axis=1))
    group = lax.axis_index("bands")
    for at in range(len(blocks)):
        target = 0
        for stride, radix in digits(len(blocks)):
            target = target + (group // stride + at // stride) % radix * stride
        gram[target] = jnp.transpose(product[:, at * width : (at + 1) * width]).astype(BF16)


def vmem(count):
    return [pl.BlockSpec(memory_space=pltpu.VMEM)] * count


def body(wavefunctions, hamiltonians, connectivity, face_nodes):
    node_count, width = wavefunctions.shape
    shared = face_nodes.shape[1]
    padded = -(-shared // 32) * 32
    lanes = -(-node_count // 128) * 128
    parts = lax.axis_size("cells")
    groups = lax.axis_size("bands")
    place = lax.axis_index("cells")
    nodal = (node_count, width)
    shape = jax.ShapeDtypeStruct
    params = pltpu.CompilerParams(vmem_limit_bytes=24 * 2**20)

    start, local, sums, ham, one, columns = pl.pallas_call(
        first_kernel,
        out_shape=(
            shape(nodal, BF16),
            shape(nodal, F32),
            shape((2 * padded, width), BF16),
            shape(hamiltonians.shape[1:], BF16),
            shape((2 * padded, node_count), BF16),
            shape((lanes, 8), F32),
        ),
        in_specs=[pl.BlockSpec(memory_space=pltpu.HBM)] * 4,
        out_specs=tuple(vmem(6)),
        scratch_shapes=[
            pltpu.VMEM(nodal, BF16),
            pltpu.VMEM(connectivity.shape, jnp.int32),
            pltpu.VMEM(face_nodes.shape, jnp.int32),
            pltpu.VMEM((8, lanes), F32),
            pltpu.SemaphoreType.DMA((3 + len(row_chunks(node_count)),)),
        ],
        compiler_params=params,
    )(*(pltpu.with_memory_space_constraint(x, pltpu.HBM) for x in (wavefunctions, connectivity, face_nodes, hamiltonians)))

    both = ("cells", "bands")
    chip = digits(groups)[-1] if groups > 1 else (1, 1)

    def pair_swap(first):
        pairs = []
        for part in range(parts):
            other = first + ((part - first) ^ 1)
            for band in range(groups):
                if part >= first and other < parts:
                    pairs.append((part * groups + band, other * groups + band))
                else:
                    pairs.append((part * groups + band, part * groups + turn(band, *chip, 1)))
        return pairs

    odd = place % 2 == 1
    even = place % 2 == 0

    def neighbours(sums):
        low, high = sums[:padded], sums[padded:]
        even_odd = lax.ppermute(jnp.where(odd, low, high), both, pair_swap(0))
        odd_even = lax.ppermute(jnp.where(odd, high, low), both, pair_swap(1))
        return jnp.where(even, odd_even, even_odd), jnp.where(even, even_odd, odd_even)

    before, after = neighbours(sums)
    one_t, keep, mine, border = pl.pallas_call(
        middle_kernel,
        out_shape=(
            shape((node_count, 2 * padded), BF16),
            shape(nodal, F32),
            shape(nodal, F32),
            shape((node_count, 2 * padded), BF16),
        ),
        in_specs=vmem(4),
        out_specs=tuple(vmem(4)),
        compiler_params=params,
    )(columns, face_nodes, local, ham)
    result, block = pl.pallas_call(
        second_kernel,
        out_shape=(shape(nodal, F32), shape(nodal, BF16)),
        in_specs=vmem(6),
        out_specs=tuple(vmem(2)),
        compiler_params=params,
    )(before, after, mine, border, start, keep)

    blocks = {0: block}
    for stride, radix in reversed(digits(groups)):
        for at in list(blocks):
            for by in range(1, radix):
                blocks[at + by * stride] = lax.ppermute(blocks[at], "bands", turned(groups, stride, radix, radix - by))
    sums = pl.pallas_call(
        face_kernel,
        out_shape=shape((2 * padded, 2 * width), BF16),
        in_specs=vmem(3),
        out_specs=vmem(1)[0],
        compiler_params=params,
    )(result, start, one)
    before, after = neighbours(sums)
    filtered, gram = pl.pallas_call(
        third_kernel,
        out_shape=(shape(nodal, F32), shape((groups, width, width), BF16)),
        in_specs=vmem(6 + groups),
        out_specs=tuple(vmem(2)),
        compiler_params=params,
    )(result, start, keep, before, after, one_t, *(blocks[at] for at in range(groups)))
    total = sum_over_cells(gram) * (1.0 / (parts * node_count))
    correlation = total.reshape(groups * width, width)

    place_of = (lax.broadcasted_iota(jnp.int32, (node_count, node_count), 0) == connectivity).astype(BF16)
    top = filtered.astype(BF16)
    rest = filtered - top.astype(F32)
    middle = rest.astype(BF16)
    small = (rest - middle.astype(F32)).astype(BF16)
    return dot(place_of, small) + dot(place_of, middle) + dot(place_of, top), correlation


def solution(mesh):
    placed = (P("cells", "bands"), P("cells", None, None), P("cells", None), P("cells", None))
    return jax.shard_map(
        body,
        mesh=mesh,
        in_specs=placed,
        out_specs=(P("cells", "bands"), P(None, "bands")),
        check_vma=False,
    )
```

```python
import jax
import jax.numpy as jnp
from jax import lax
from jax.experimental import pallas as pl
from jax.experimental.pallas import tpu as pltpu
from jax.sharding import PartitionSpec as P

BF16 = jnp.bfloat16
F32 = jnp.float32


def digits(count):
    stride, left, out = 1, count, []
    for radix in range(2, count + 1):
        while left % radix == 0:
            out.append((stride, radix))
            stride *= radix
            left //= radix
    return out


def turn(index, stride, radix, by):
    digit = index // stride % radix
    return index + ((digit + by) % radix - digit) * stride


def turned(count, stride, radix, by):
    return [(source, turn(source, stride, radix, by)) for source in range(count)]


def sum_over_cells(value):
    parts, groups = lax.axis_size("cells"), lax.axis_size("bands")
    binary = [stride for stride, radix in digits(parts) if radix == 2]
    other = [(stride, radix) for stride, radix in digits(parts) if radix != 2]
    masks = [stride + (stride // 2 if stride > 2 else 0) for stride in binary]
    steps = []
    if len(masks) >= 2:
        first, second = masks[:2]
        steps.append([(first, second), (second, first), (first ^ second, first ^ second)])
        masks = masks[2:]
    steps += [[(mask, mask)] for mask in masks]
    steps = [[lambda part, band, m=m: part ^ m[band % 2] for m in step] for step in steps]
    for stride, radix in other:
        steps.append([lambda part, band, d=(stride, radix, by): turn(part, *d) for by in range(1, radix)])
    kind = BF16 if len(steps) <= 3 else F32
    for step in steps:
        word = value.astype(kind)
        words = [word.astype(F32)]
        for move in step:
            pairs = [
                (part * groups + band, move(part, band) * groups + band) for part in range(parts) for band in range(groups)
            ]
            words.append(lax.ppermute(word, ("cells", "bands"), pairs).astype(F32))
        value = words[0] + words[1]
        if len(words) == 4:
            value = value + (words[2] + words[3])
        elif len(words) == 3:
            value = value + words[2]
    return value


def dot(a, b):
    return jnp.dot(a, b, preferred_element_type=F32)


def dot_t(a, b):
    return lax.dot_general(a, b, (((0,), (0,)), ((), ())), preferred_element_type=F32)


def one_hot(flags):
    return jnp.where(flags, jnp.float32(1), jnp.float32(0)).astype(BF16)


def row_chunks(count):
    return [(first, min(first + 368, count)) for first in range(0, count, 368)]


def tall_dot(rows_of, values, count=None):
    chunks = row_chunks(count or values.shape[0])
    return jnp.concatenate([dot(rows_of(first, last), values) for first, last in chunks], axis=0)


def first_kernel(waves_hbm, cell_hbm, faces_hbm, ham_hbm, start, local, sums, ham, one, columns, waves, cell, faces, rows, sems):
    count = waves.shape[0]
    shared = faces.shape[1]
    padded = one.shape[0] // 2
    pairs = ((cell_hbm, cell), (faces_hbm, faces), (waves_hbm, waves), (ham_hbm.at[0], ham))
    copies = [pltpu.make_async_copy(source, target, sems.at[at]) for at, (source, target) in enumerate(pairs)]
    for copy in copies:
        copy.start()
    rows[...] = jnp.full(rows.shape, -1, F32)
    copies[0].wait()
    copies[1].wait()
    row = cell[...].astype(F32)
    rows[0:1, :count] = row
    rows[1:3, :shared] = faces[...].astype(F32)
    turned_rows = jnp.transpose(rows[...])
    columns[...] = turned_rows
    nodes = lax.broadcasted_iota(jnp.int32, (count, count), 1).astype(F32)
    place = one_hot(turned_rows[:count, 0:1] == nodes)
    copies[2].wait()
    begin = tall_dot(lambda first, last: place[first:last], waves[...]).astype(BF16)
    start[...] = begin
    pick = one_hot(jnp.concatenate([turned_rows[:padded, 1:2], turned_rows[:padded, 2:3]], axis=0) == row)
    one[...] = pick
    copies[3].wait()
    local[...] = tall_dot(lambda first, last: ham[first:last], begin)
    sums[...] = dot(pick, local[...].astype(BF16)).astype(BF16)


def middle_kernel(columns, faces, local, ham, one_t, keep, mine, border):
    count = one_t.shape[0]
    shared = faces.shape[1]
    padded = one_t.shape[1] // 2
    col = columns[:count, 0:1]
    row = faces[...].astype(F32)
    part, parts = lax.axis_index("cells"), lax.axis_size("cells")
    has_before = jnp.where(part > 0, jnp.float32(1), jnp.float32(0))
    has_after = jnp.where(part < parts - 1, jnp.float32(1), jnp.float32(0))
    first = jnp.where(col == row[0:1], jnp.float32(1), jnp.float32(0))
    second = jnp.where(col == row[1:2], jnp.float32(1), jnp.float32(0))
    one_t[...] = jnp.zeros(one_t.shape, BF16)
    one_t[:, :shared] = (first * has_before).astype(BF16)
    one_t[:, padded : padded + shared] = (second * has_after).astype(BF16)
    keep[...] = jnp.broadcast_to(1.0 - jnp.sum(first, axis=1, keepdims=True) * has_before, keep.shape)
    half = (0.5 * local[...]).astype(BF16)
    both = tall_dot(lambda first, last: ham[first:last], jnp.concatenate([half, one_t[...]], axis=1))
    width = local.shape[1]
    mine[...] = both[:, :width]
    border[...] = both[:, width:].astype(BF16)


def second_kernel(before, after, mine, border, start, keep, result, block):
    halo = 0.5 * jnp.concatenate([before[...], after[...]], axis=0).astype(F32)
    sums = mine[...] + tall_dot(lambda first, last: border[first:last], halo.astype(BF16), border.shape[0])
    result[...] = sums
    block[...] = (sums - start[...].astype(F32) * keep[...]).astype(BF16)


def face_kernel(result, start, one, sums):
    sums[...] = dot(one[...], jnp.concatenate([result[...].astype(BF16), start[...]], axis=1)).astype(BF16)


def third_kernel(result, start, keep, before, after, one_t, *rest):
    blocks, (filtered, gram) = rest[:-2], rest[-2:]
    width = result.shape[1]
    here = jnp.concatenate([before[:, :width], after[:, :width]], axis=0)
    there = jnp.concatenate([before[:, width:], jnp.zeros((after.shape[0], width), BF16)], axis=0)
    halo_in = jnp.concatenate([here, there], axis=1)
    halo = tall_dot(lambda first, last: one_t[first:last], halo_in, one_t.shape[0])
    older = start[...].astype(F32)
    whole = result[...] + halo[:, :width]
    filtered[...] = whole - older
    right = (whole - older * keep[...] - halo[:, width:]).astype(BF16)
    product = dot_t(right, jnp.concatenate([block[...] for block in blocks], axis=1))
    group = lax.axis_index("bands")
    for at in range(len(blocks)):
        target = 0
        for stride, radix in digits(len(blocks)):
            target = target + (group // stride + at // stride) % radix * stride
        gram[target] = jnp.transpose(product[:, at * width : (at + 1) * width]).astype(BF16)


def vmem(count):
    return [pl.BlockSpec(memory_space=pltpu.VMEM)] * count


def body(wavefunctions, hamiltonians, connectivity, face_nodes):
    node_count, width = wavefunctions.shape
    shared = face_nodes.shape[1]
    padded = -(-shared // 32) * 32
    lanes = -(-node_count // 128) * 128
    parts = lax.axis_size("cells")
    groups = lax.axis_size("bands")
    place = lax.axis_index("cells")
    nodal = (node_count, width)
    shape = jax.ShapeDtypeStruct
    params = pltpu.CompilerParams(vmem_limit_bytes=24 * 2**20)

    start, local, sums, ham, one, columns = pl.pallas_call(
        first_kernel,
        out_shape=(
            shape(nodal, BF16),
            shape(nodal, F32),
            shape((2 * padded, width), BF16),
            shape(hamiltonians.shape[1:], BF16),
            shape((2 * padded, node_count), BF16),
            shape((lanes, 8), F32),
        ),
        in_specs=[pl.BlockSpec(memory_space=pltpu.HBM)] * 4,
        out_specs=tuple(vmem(6)),
        scratch_shapes=[
            pltpu.VMEM(nodal, BF16),
            pltpu.VMEM(connectivity.shape, jnp.int32),
            pltpu.VMEM(face_nodes.shape, jnp.int32),
            pltpu.VMEM((8, lanes), F32),
            pltpu.SemaphoreType.DMA((4,)),
        ],
        compiler_params=params,
    )(*(pltpu.with_memory_space_constraint(x, pltpu.HBM) for x in (wavefunctions, connectivity, face_nodes, hamiltonians)))

    both = ("cells", "bands")
    chip = digits(groups)[-1] if groups > 1 else (1, 1)

    def pair_swap(first):
        pairs = []
        for part in range(parts):
            other = first + ((part - first) ^ 1)
            for band in range(groups):
                if part >= first and other < parts:
                    pairs.append((part * groups + band, other * groups + band))
                else:
                    pairs.append((part * groups + band, part * groups + turn(band, *chip, 1)))
        return pairs

    odd = place % 2 == 1
    even = place % 2 == 0

    def neighbours(sums):
        low, high = sums[:padded], sums[padded:]
        even_odd = lax.ppermute(jnp.where(odd, low, high), both, pair_swap(0))
        odd_even = lax.ppermute(jnp.where(odd, high, low), both, pair_swap(1))
        return jnp.where(even, odd_even, even_odd), jnp.where(even, even_odd, odd_even)

    before, after = neighbours(sums)
    one_t, keep, mine, border = pl.pallas_call(
        middle_kernel,
        out_shape=(
            shape((node_count, 2 * padded), BF16),
            shape(nodal, F32),
            shape(nodal, F32),
            shape((node_count, 2 * padded), BF16),
        ),
        in_specs=vmem(4),
        out_specs=tuple(vmem(4)),
        compiler_params=params,
    )(columns, face_nodes, local, ham)
    result, block = pl.pallas_call(
        second_kernel,
        out_shape=(shape(nodal, F32), shape(nodal, BF16)),
        in_specs=vmem(6),
        out_specs=tuple(vmem(2)),
        compiler_params=params,
    )(before, after, mine, border, start, keep)

    blocks = {0: block}
    for stride, radix in reversed(digits(groups)):
        for at in list(blocks):
            for by in range(1, radix):
                blocks[at + by * stride] = lax.ppermute(blocks[at], "bands", turned(groups, stride, radix, radix - by))
    sums = pl.pallas_call(
        face_kernel,
        out_shape=shape((2 * padded, 2 * width), BF16),
        in_specs=vmem(3),
        out_specs=vmem(1)[0],
        compiler_params=params,
    )(result, start, one)
    before, after = neighbours(sums)
    filtered, gram = pl.pallas_call(
        third_kernel,
        out_shape=(shape(nodal, F32), shape((groups, width, width), BF16)),
        in_specs=vmem(6 + groups),
        out_specs=tuple(vmem(2)),
        compiler_params=params,
    )(result, start, keep, before, after, one_t, *(blocks[at] for at in range(groups)))
    total = sum_over_cells(gram) * (1.0 / (parts * node_count))
    correlation = total.reshape(groups * width, width)

    place_of = (lax.broadcasted_iota(jnp.int32, (node_count, node_count), 0) == connectivity).astype(BF16)
    top = filtered.astype(BF16)
    rest = filtered - top.astype(F32)
    middle = rest.astype(BF16)
    small = (rest - middle.astype(F32)).astype(BF16)
    return dot(place_of, small) + dot(place_of, middle) + dot(place_of, top), correlation


def solution(mesh):
    placed = (P("cells", "bands"), P("cells", None, None), P("cells", None), P("cells", None))
    return jax.shard_map(
        body,
        mesh=mesh,
        in_specs=placed,
        out_specs=(P("cells", "bands"), P(None, "bands")),
        check_vma=False,
    )
```

```python
import jax
import jax.numpy as jnp
from jax import lax
from jax.experimental import pallas as pl
from jax.experimental.pallas import tpu as pltpu
from jax.sharding import PartitionSpec as P

BF16 = jnp.bfloat16
F32 = jnp.float32


def digits(count):
    stride, left, out = 1, count, []
    for radix in range(2, count + 1):
        while left % radix == 0:
            out.append((stride, radix))
            stride *= radix
            left //= radix
    return out


def turn(index, stride, radix, by):
    digit = index // stride % radix
    return index + ((digit + by) % radix - digit) * stride


def turned(count, stride, radix, by):
    return [(source, turn(source, stride, radix, by)) for source in range(count)]


def sum_over_cells(value):
    parts, groups = lax.axis_size("cells"), lax.axis_size("bands")
    binary = [stride for stride, radix in digits(parts) if radix == 2]
    other = [(stride, radix) for stride, radix in digits(parts) if radix != 2]
    masks = [stride + (stride // 2 if stride > 2 else 0) for stride in binary]
    steps = []
    if len(masks) >= 2:
        first, second = masks[:2]
        steps.append([(first, second), (second, first), (first ^ second, first ^ second)])
        masks = masks[2:]
    steps += [[(mask, mask)] for mask in masks]
    steps = [[lambda part, band, m=m: part ^ m[band % 2] for m in step] for step in steps]
    for stride, radix in other:
        steps.append([lambda part, band, d=(stride, radix, by): turn(part, *d) for by in range(1, radix)])
    kind = BF16 if len(steps) <= 3 else F32
    for step in steps:
        word = value.astype(kind)
        words = [word.astype(F32)]
        for move in step:
            pairs = [
                (part * groups + band, move(part, band) * groups + band) for part in range(parts) for band in range(groups)
            ]
            words.append(lax.ppermute(word, ("cells", "bands"), pairs).astype(F32))
        value = words[0] + words[1]
        if len(words) == 4:
            value = value + (words[2] + words[3])
        elif len(words) == 3:
            value = value + words[2]
    return value


def dot(a, b):
    return jnp.dot(a, b, preferred_element_type=F32)


def dot_t(a, b):
    return lax.dot_general(a, b, (((0,), (0,)), ((), ())), preferred_element_type=F32)


def one_hot(flags):
    return jnp.where(flags, jnp.float32(1), jnp.float32(0)).astype(BF16)


def row_chunks(count):
    return [(first, min(first + 368, count)) for first in range(0, count, 368)]


def tall_dot(rows_of, values, count=None):
    chunks = row_chunks(count or values.shape[0])
    return jnp.concatenate([dot(rows_of(first, last), values) for first, last in chunks], axis=0)


def first_kernel(waves_hbm, cell_hbm, faces_hbm, ham_hbm, start, local, sums, ham, one, columns, waves, cell, faces, rows, sems):
    count = waves.shape[0]
    shared = faces.shape[1]
    padded = one.shape[0] // 2
    pairs = ((cell_hbm, cell), (faces_hbm, faces), (waves_hbm, waves), (ham_hbm.at[0], ham))
    copies = [pltpu.make_async_copy(source, target, sems.at[at]) for at, (source, target) in enumerate(pairs)]
    for copy in copies:
        copy.start()
    rows[...] = jnp.full(rows.shape, -1, F32)
    copies[0].wait()
    copies[1].wait()
    row = cell[...].astype(F32)
    rows[0:1, :count] = row
    rows[1:3, :shared] = faces[...].astype(F32)
    turned_rows = jnp.transpose(rows[...])
    columns[...] = turned_rows
    nodes = lax.broadcasted_iota(jnp.int32, (count, count), 1).astype(F32)
    place = one_hot(turned_rows[:count, 0:1] == nodes)
    copies[2].wait()
    begin = tall_dot(lambda first, last: place[first:last], waves[...]).astype(BF16)
    start[...] = begin
    pick = one_hot(jnp.concatenate([turned_rows[:padded, 1:2], turned_rows[:padded, 2:3]], axis=0) == row)
    one[...] = pick
    copies[3].wait()
    local[...] = tall_dot(lambda first, last: ham[first:last], begin)
    sums[...] = dot(pick, local[...].astype(BF16)).astype(BF16)


def middle_kernel(columns, faces, local, ham, one_t, keep, mine, border):
    count = one_t.shape[0]
    shared = faces.shape[1]
    padded = one_t.shape[1] // 2
    col = columns[:count, 0:1]
    row = faces[...].astype(F32)
    part, parts = lax.axis_index("cells"), lax.axis_size("cells")
    has_before = jnp.where(part > 0, jnp.float32(1), jnp.float32(0))
    has_after = jnp.where(part < parts - 1, jnp.float32(1), jnp.float32(0))
    first = jnp.where(col == row[0:1], jnp.float32(1), jnp.float32(0))
    second = jnp.where(col == row[1:2], jnp.float32(1), jnp.float32(0))
    one_t[...] = jnp.zeros(one_t.shape, BF16)
    one_t[:, :shared] = (first * has_before).astype(BF16)
    one_t[:, padded : padded + shared] = (second * has_after).astype(BF16)
    keep[...] = jnp.broadcast_to(1.0 - jnp.sum(first, axis=1, keepdims=True) * has_before, keep.shape)
    half = (0.5 * local[...]).astype(BF16)
    both = tall_dot(lambda first, last: ham[first:last], jnp.concatenate([half, one_t[...]], axis=1))
    width = local.shape[1]
    mine[...] = both[:, :width]
    border[...] = both[:, width:].astype(BF16)


def second_kernel(before, after, mine, border, start, keep, result, block):
    halo = 0.5 * jnp.concatenate([before[...], after[...]], axis=0).astype(F32)
    sums = mine[...] + tall_dot(lambda first, last: border[first:last], halo.astype(BF16), border.shape[0])
    result[...] = sums
    block[...] = (sums - start[...].astype(F32) * keep[...]).astype(BF16)


def face_kernel(result, start, one, sums):
    sums[...] = dot(one[...], jnp.concatenate([result[...].astype(BF16), start[...]], axis=1)).astype(BF16)


def third_kernel(result, start, keep, before, after, one_t, *rest):
    blocks, (filtered, gram) = rest[:-2], rest[-2:]
    width = result.shape[1]
    here = jnp.concatenate([before[:, :width], after[:, :width]], axis=0)
    there = jnp.concatenate([before[:, width:], jnp.zeros((after.shape[0], width), BF16)], axis=0)
    halo_in = jnp.concatenate([here, there], axis=1)
    halo = tall_dot(lambda first, last: one_t[first:last], halo_in, one_t.shape[0])
    older = start[...].astype(F32)
    whole = result[...] + halo[:, :width]
    filtered[...] = whole - older
    right = (whole - older * keep[...] - halo[:, width:]).astype(BF16)
    product = dot_t(right, jnp.concatenate([block[...] for block in blocks], axis=1))
    group = lax.axis_index("bands")
    for at in range(len(blocks)):
        target = 0
        for stride, radix in digits(len(blocks)):
            target = target + (group // stride + at // stride) % radix * stride
        gram[target] = jnp.transpose(product[:, at * width : (at + 1) * width]).astype(BF16)


def vmem(count):
    return [pl.BlockSpec(memory_space=pltpu.VMEM)] * count


def body(wavefunctions, hamiltonians, connectivity, face_nodes):
    node_count, width = wavefunctions.shape
    shared = face_nodes.shape[1]
    padded = -(-shared // 32) * 32
    lanes = -(-node_count // 128) * 128
    parts = lax.axis_size("cells")
    groups = lax.axis_size("bands")
    place = lax.axis_index("cells")
    nodal = (node_count, width)
    shape = jax.ShapeDtypeStruct
    params = pltpu.CompilerParams(vmem_limit_bytes=24 * 2**20)

    start, local, sums, ham, one, columns = pl.pallas_call(
        first_kernel,
        out_shape=(
            shape(nodal, BF16),
            shape(nodal, F32),
            shape((2 * padded, width), BF16),
            shape(hamiltonians.shape[1:], BF16),
            shape((2 * padded, node_count), BF16),
            shape((lanes, 8), F32),
        ),
        in_specs=[pl.BlockSpec(memory_space=pltpu.HBM)] * 4,
        out_specs=tuple(vmem(6)),
        scratch_shapes=[
            pltpu.VMEM(nodal, BF16),
            pltpu.VMEM(connectivity.shape, jnp.int32),
            pltpu.VMEM(face_nodes.shape, jnp.int32),
            pltpu.VMEM((8, lanes), F32),
            pltpu.SemaphoreType.DMA((4,)),
        ],
        compiler_params=params,
    )(*(pltpu.with_memory_space_constraint(x, pltpu.HBM) for x in (wavefunctions, connectivity, face_nodes, hamiltonians)))

    both = ("cells", "bands")
    core, chip = (digits(groups)[0], digits(groups)[-1]) if groups > 1 else ((1, 1), (1, 1))

    def pair_swap(first, spare):
        pairs = []
        for part in range(parts):
            other = first + ((part - first) ^ 1)
            for band in range(groups):
                if part >= first and other < parts:
                    pairs.append((part * groups + band, other * groups + band))
                else:
                    pairs.append((part * groups + band, part * groups + turn(band, *spare, 1)))
        return pairs

    odd = place % 2 == 1
    even = place % 2 == 0

    def neighbours(sums, spare):
        low, high = sums[:padded], sums[padded:]
        even_odd = lax.ppermute(jnp.where(odd, low, high), both, pair_swap(0, spare))
        odd_even = lax.ppermute(jnp.where(odd, high, low), both, pair_swap(1, spare))
        return jnp.where(even, odd_even, even_odd), jnp.where(even, even_odd, odd_even)

    before, after = neighbours(sums, core)
    one_t, keep, mine, border = pl.pallas_call(
        middle_kernel,
        out_shape=(
            shape((node_count, 2 * padded), BF16),
            shape(nodal, F32),
            shape(nodal, F32),
            shape((node_count, 2 * padded), BF16),
        ),
        in_specs=vmem(4),
        out_specs=tuple(vmem(4)),
        compiler_params=params,
    )(columns, face_nodes, local, ham)
    result, block = pl.pallas_call(
        second_kernel,
        out_shape=(shape(nodal, F32), shape(nodal, BF16)),
        in_specs=vmem(6),
        out_specs=tuple(vmem(2)),
        compiler_params=params,
    )(before, after, mine, border, start, keep)

    blocks = {0: block}
    for stride, radix in reversed(digits(groups)):
        for at in list(blocks):
            for by in range(1, radix):
                blocks[at + by * stride] = lax.ppermute(blocks[at], "bands", turned(groups, stride, radix, radix - by))
    sums = pl.pallas_call(
        face_kernel,
        out_shape=shape((2 * padded, 2 * width), BF16),
        in_specs=vmem(3),
        out_specs=vmem(1)[0],
        compiler_params=params,
    )(result, start, one)
    before, after = neighbours(sums, chip)
    filtered, gram = pl.pallas_call(
        third_kernel,
        out_shape=(shape(nodal, F32), shape((groups, width, width), BF16)),
        in_specs=vmem(6 + groups),
        out_specs=tuple(vmem(2)),
        compiler_params=params,
    )(result, start, keep, before, after, one_t, *(blocks[at] for at in range(groups)))
    total = sum_over_cells(gram) * (1.0 / (parts * node_count))
    correlation = total.reshape(groups * width, width)

    place_of = (lax.broadcasted_iota(jnp.int32, (node_count, node_count), 0) == connectivity).astype(BF16)
    top = filtered.astype(BF16)
    rest = filtered - top.astype(F32)
    middle = rest.astype(BF16)
    small = (rest - middle.astype(F32)).astype(BF16)
    return dot(place_of, small) + dot(place_of, middle) + dot(place_of, top), correlation


def solution(mesh):
    placed = (P("cells", "bands"), P("cells", None, None), P("cells", None), P("cells", None))
    return jax.shard_map(
        body,
        mesh=mesh,
        in_specs=placed,
        out_specs=(P("cells", "bands"), P(None, "bands")),
        check_vma=False,
    )
```

```python
import jax
import jax.numpy as jnp
from jax import lax
from jax.experimental import pallas as pl
from jax.experimental.pallas import tpu as pltpu
from jax.sharding import PartitionSpec as P

BF16 = jnp.bfloat16
F32 = jnp.float32


def digits(count):
    stride, left, out = 1, count, []
    for radix in range(2, count + 1):
        while left % radix == 0:
            out.append((stride, radix))
            stride *= radix
            left //= radix
    return out


def turn(index, stride, radix, by):
    digit = index // stride % radix
    return index + ((digit + by) % radix - digit) * stride


def turned(count, stride, radix, by):
    return [(source, turn(source, stride, radix, by)) for source in range(count)]


def sum_over_cells(value):
    parts, groups = lax.axis_size("cells"), lax.axis_size("bands")
    binary = [stride for stride, radix in digits(parts) if radix == 2]
    other = [(stride, radix) for stride, radix in digits(parts) if radix != 2]
    masks = [stride + (stride // 2 if stride > 2 else 0) for stride in binary]
    steps = []
    if len(masks) >= 2:
        first, second = masks[:2]
        steps.append([(first, second), (second, first), (first ^ second, first ^ second)])
        masks = masks[2:]
    steps += [[(mask, mask)] for mask in masks]
    steps = [[lambda part, band, m=m: part ^ m[band % 2] for m in step] for step in steps]
    for stride, radix in other:
        steps.append([lambda part, band, d=(stride, radix, by): turn(part, *d) for by in range(1, radix)])
    kind = BF16 if len(steps) <= 3 else F32
    for step in steps:
        word = value.astype(kind)
        words = [word.astype(F32)]
        for move in step:
            pairs = [
                (part * groups + band, move(part, band) * groups + band) for part in range(parts) for band in range(groups)
            ]
            words.append(lax.ppermute(word, ("cells", "bands"), pairs).astype(F32))
        value = words[0] + words[1]
        if len(words) == 4:
            value = value + (words[2] + words[3])
        elif len(words) == 3:
            value = value + words[2]
    return value


def dot(a, b):
    return jnp.dot(a, b, preferred_element_type=F32)


def dot_t(a, b):
    return lax.dot_general(a, b, (((0,), (0,)), ((), ())), preferred_element_type=F32)


def one_hot(flags):
    return jnp.where(flags, jnp.float32(1), jnp.float32(0)).astype(BF16)


def row_chunks(count):
    return [(first, min(first + 368, count)) for first in range(0, count, 368)]


def tall_dot(rows_of, values, count=None):
    chunks = row_chunks(count or values.shape[0])
    return jnp.concatenate([dot(rows_of(first, last), values) for first, last in chunks], axis=0)


def first_kernel(waves_hbm, cell_hbm, faces_hbm, ham_hbm, start, local, sums, ham, one, columns, waves, cell, faces, rows, sems):
    count = waves.shape[0]
    shared = faces.shape[1]
    padded = one.shape[0] // 2
    pairs = ((cell_hbm, cell), (faces_hbm, faces), (waves_hbm, waves), (ham_hbm.at[0], ham))
    copies = [pltpu.make_async_copy(source, target, sems.at[at]) for at, (source, target) in enumerate(pairs)]
    for copy in copies:
        copy.start()
    rows[...] = jnp.full(rows.shape, -1, F32)
    copies[0].wait()
    copies[1].wait()
    row = cell[...].astype(F32)
    rows[0:1, :count] = row
    rows[1:3, :shared] = faces[...].astype(F32)
    turned_rows = jnp.transpose(rows[...])
    columns[...] = turned_rows
    nodes = lax.broadcasted_iota(jnp.int32, (count, count), 1).astype(F32)
    place = one_hot(turned_rows[:count, 0:1] == nodes)
    copies[2].wait()
    begin = tall_dot(lambda first, last: place[first:last], waves[...]).astype(BF16)
    start[...] = begin
    pick = one_hot(jnp.concatenate([turned_rows[:padded, 1:2], turned_rows[:padded, 2:3]], axis=0) == row)
    one[...] = pick
    copies[3].wait()
    local[...] = tall_dot(lambda first, last: ham[first:last], begin)
    sums[...] = dot(pick, local[...].astype(BF16)).astype(BF16)


def middle_kernel(columns, faces, local, ham, one_t, keep, mine, border):
    count = one_t.shape[0]
    shared = faces.shape[1]
    padded = one_t.shape[1] // 2
    col = columns[:count, 0:1]
    row = faces[...].astype(F32)
    part, parts = lax.axis_index("cells"), lax.axis_size("cells")
    has_before = jnp.where(part > 0, jnp.float32(1), jnp.float32(0))
    has_after = jnp.where(part < parts - 1, jnp.float32(1), jnp.float32(0))
    first = jnp.where(col == row[0:1], jnp.float32(1), jnp.float32(0))
    second = jnp.where(col == row[1:2], jnp.float32(1), jnp.float32(0))
    one_t[...] = jnp.zeros(one_t.shape, BF16)
    one_t[:, :shared] = (first * has_before).astype(BF16)
    one_t[:, padded : padded + shared] = (second * has_after).astype(BF16)
    keep[...] = jnp.broadcast_to(1.0 - jnp.sum(first, axis=1, keepdims=True) * has_before, keep.shape)
    half = (0.5 * local[...]).astype(BF16)
    both = tall_dot(lambda first, last: ham[first:last], jnp.concatenate([half, one_t[...]], axis=1))
    width = local.shape[1]
    mine[...] = both[:, :width]
    border[...] = both[:, width:].astype(BF16)


def second_kernel(before, after, mine, border, start, keep, result, block):
    halo = 0.5 * jnp.concatenate([before[...], after[...]], axis=0).astype(F32)
    sums = mine[...] + tall_dot(lambda first, last: border[first:last], halo.astype(BF16), border.shape[0])
    result[...] = sums
    block[...] = (sums - start[...].astype(F32) * keep[...]).astype(BF16)


def face_kernel(result, start, one, sums):
    sums[...] = dot(one[...], jnp.concatenate([result[...].astype(BF16), start[...]], axis=1)).astype(BF16)


def third_kernel(result, start, keep, before, after, one_t, *rest):
    blocks, (filtered, gram) = rest[:-2], rest[-2:]
    width = result.shape[1]
    here = jnp.concatenate([before[:, :width], after[:, :width]], axis=0)
    there = jnp.concatenate([before[:, width:], jnp.zeros((after.shape[0], width), BF16)], axis=0)
    halo_in = jnp.concatenate([here, there], axis=1)
    halo = tall_dot(lambda first, last: one_t[first:last], halo_in, one_t.shape[0])
    older = start[...].astype(F32)
    whole = result[...] + halo[:, :width]
    filtered[...] = whole - older
    right = (whole - older * keep[...] - halo[:, width:]).astype(BF16)
    left = [jnp.transpose(block[...].astype(F32)).astype(BF16) for block in blocks]
    group = lax.axis_index("bands")
    for at in range(len(blocks)):
        target = 0
        for stride, radix in digits(len(blocks)):
            target = target + (group // stride + at // stride) % radix * stride
        gram[target] = dot(left[at], right).astype(BF16)


def vmem(count):
    return [pl.BlockSpec(memory_space=pltpu.VMEM)] * count


def body(wavefunctions, hamiltonians, connectivity, face_nodes):
    node_count, width = wavefunctions.shape
    shared = face_nodes.shape[1]
    padded = -(-shared // 32) * 32
    lanes = -(-node_count // 128) * 128
    parts = lax.axis_size("cells")
    groups = lax.axis_size("bands")
    place = lax.axis_index("cells")
    nodal = (node_count, width)
    shape = jax.ShapeDtypeStruct
    params = pltpu.CompilerParams(vmem_limit_bytes=24 * 2**20)

    start, local, sums, ham, one, columns = pl.pallas_call(
        first_kernel,
        out_shape=(
            shape(nodal, BF16),
            shape(nodal, F32),
            shape((2 * padded, width), BF16),
            shape(hamiltonians.shape[1:], BF16),
            shape((2 * padded, node_count), BF16),
            shape((lanes, 8), F32),
        ),
        in_specs=[pl.BlockSpec(memory_space=pltpu.HBM)] * 4,
        out_specs=tuple(vmem(6)),
        scratch_shapes=[
            pltpu.VMEM(nodal, BF16),
            pltpu.VMEM(connectivity.shape, jnp.int32),
            pltpu.VMEM(face_nodes.shape, jnp.int32),
            pltpu.VMEM((8, lanes), F32),
            pltpu.SemaphoreType.DMA((4,)),
        ],
        compiler_params=params,
    )(*(pltpu.with_memory_space_constraint(x, pltpu.HBM) for x in (wavefunctions, connectivity, face_nodes, hamiltonians)))

    both = ("cells", "bands")
    chip = digits(groups)[-1] if groups > 1 else (1, 1)

    def pair_swap(first):
        pairs = []
        for part in range(parts):
            other = first + ((part - first) ^ 1)
            for band in range(groups):
                if part >= first and other < parts:
                    pairs.append((part * groups + band, other * groups + band))
                else:
                    pairs.append((part * groups + band, part * groups + turn(band, *chip, 1)))
        return pairs

    odd = place % 2 == 1
    even = place % 2 == 0

    def neighbours(sums):
        low, high = sums[:padded], sums[padded:]
        even_odd = lax.ppermute(jnp.where(odd, low, high), both, pair_swap(0))
        odd_even = lax.ppermute(jnp.where(odd, high, low), both, pair_swap(1))
        return jnp.where(even, odd_even, even_odd), jnp.where(even, even_odd, odd_even)

    before, after = neighbours(sums)
    one_t, keep, mine, border = pl.pallas_call(
        middle_kernel,
        out_shape=(
            shape((node_count, 2 * padded), BF16),
            shape(nodal, F32),
            shape(nodal, F32),
            shape((node_count, 2 * padded), BF16),
        ),
        in_specs=vmem(4),
        out_specs=tuple(vmem(4)),
        compiler_params=params,
    )(columns, face_nodes, local, ham)
    result, block = pl.pallas_call(
        second_kernel,
        out_shape=(shape(nodal, F32), shape(nodal, BF16)),
        in_specs=vmem(6),
        out_specs=tuple(vmem(2)),
        compiler_params=params,
    )(before, after, mine, border, start, keep)

    blocks = {0: block}
    for stride, radix in reversed(digits(groups)):
        for at in list(blocks):
            for by in range(1, radix):
                blocks[at + by * stride] = lax.ppermute(blocks[at], "bands", turned(groups, stride, radix, radix - by))
    sums = pl.pallas_call(
        face_kernel,
        out_shape=shape((2 * padded, 2 * width), BF16),
        in_specs=vmem(3),
        out_specs=vmem(1)[0],
        compiler_params=params,
    )(result, start, one)
    before, after = neighbours(sums)
    filtered, gram = pl.pallas_call(
        third_kernel,
        out_shape=(shape(nodal, F32), shape((groups, width, width), BF16)),
        in_specs=vmem(6 + groups),
        out_specs=tuple(vmem(2)),
        compiler_params=params,
    )(result, start, keep, before, after, one_t, *(blocks[at] for at in range(groups)))
    total = sum_over_cells(gram) * (1.0 / (parts * node_count))
    correlation = total.reshape(groups * width, width)

    place_of = (lax.broadcasted_iota(jnp.int32, (node_count, node_count), 0) == connectivity).astype(BF16)
    top = filtered.astype(BF16)
    rest = filtered - top.astype(F32)
    middle = rest.astype(BF16)
    small = (rest - middle.astype(F32)).astype(BF16)
    return dot(place_of, small) + dot(place_of, middle) + dot(place_of, top), correlation


def solution(mesh):
    placed = (P("cells", "bands"), P("cells", None, None), P("cells", None), P("cells", None))
    return jax.shard_map(
        body,
        mesh=mesh,
        in_specs=placed,
        out_specs=(P("cells", "bands"), P(None, "bands")),
        check_vma=False,
    )
```

```python
import jax
import jax.numpy as jnp
from jax import lax
from jax.experimental import pallas as pl
from jax.experimental.pallas import tpu as pltpu
from jax.sharding import PartitionSpec as P

BF16 = jnp.bfloat16
F32 = jnp.float32


def digits(count):
    stride, left, out = 1, count, []
    for radix in range(2, count + 1):
        while left % radix == 0:
            out.append((stride, radix))
            stride *= radix
            left //= radix
    return out


def turn(index, stride, radix, by):
    digit = index // stride % radix
    return index + ((digit + by) % radix - digit) * stride


def turned(count, stride, radix, by):
    return [(source, turn(source, stride, radix, by)) for source in range(count)]


def sum_over_cells(value):
    parts, groups = lax.axis_size("cells"), lax.axis_size("bands")
    binary = [stride for stride, radix in digits(parts) if radix == 2]
    other = [(stride, radix) for stride, radix in digits(parts) if radix != 2]
    masks = [stride + (stride // 2 if stride > 2 else 0) for stride in binary]
    steps = []
    if len(masks) >= 2:
        first, second = masks[:2]
        steps.append([(first, second), (second, first), (first ^ second, first ^ second)])
        masks = masks[2:]
    steps += [[(mask, mask)] for mask in masks]
    steps = [[lambda part, band, m=m: part ^ m[band % 2] for m in step] for step in steps]
    for stride, radix in other:
        steps.append([lambda part, band, d=(stride, radix, by): turn(part, *d) for by in range(1, radix)])
    kind = BF16 if len(steps) <= 3 else F32
    for step in steps:
        word = value.astype(kind)
        words = [word.astype(F32)]
        for move in step:
            pairs = [
                (part * groups + band, move(part, band) * groups + band) for part in range(parts) for band in range(groups)
            ]
            words.append(lax.ppermute(word, ("cells", "bands"), pairs).astype(F32))
        value = words[0] + words[1]
        if len(words) == 4:
            value = value + (words[2] + words[3])
        elif len(words) == 3:
            value = value + words[2]
    return value


def dot(a, b):
    return jnp.dot(a, b, preferred_element_type=F32)


def dot_t(a, b):
    return lax.dot_general(a, b, (((0,), (0,)), ((), ())), preferred_element_type=F32)


def one_hot(flags):
    return jnp.where(flags, jnp.float32(1), jnp.float32(0)).astype(BF16)


def row_chunks(count):
    return [(first, min(first + 368, count)) for first in range(0, count, 368)]


def tall_dot(rows_of, values, count=None):
    chunks = row_chunks(count or values.shape[0])
    return jnp.concatenate([dot(rows_of(first, last), values) for first, last in chunks], axis=0)


def first_kernel(waves_hbm, cell_hbm, faces_hbm, ham_hbm, start, local, sums, ham, one, columns, waves, cell, faces, rows, sems):
    count = waves.shape[0]
    shared = faces.shape[1]
    padded = one.shape[0] // 2
    pairs = ((cell_hbm, cell), (faces_hbm, faces), (waves_hbm, waves), (ham_hbm.at[0], ham))
    copies = [pltpu.make_async_copy(source, target, sems.at[at]) for at, (source, target) in enumerate(pairs)]
    for copy in copies:
        copy.start()
    rows[...] = jnp.full(rows.shape, -1, F32)
    copies[0].wait()
    copies[1].wait()
    row = cell[...].astype(F32)
    rows[0:1, :count] = row
    rows[1:3, :shared] = faces[...].astype(F32)
    turned_rows = jnp.transpose(rows[...])
    columns[...] = turned_rows
    nodes = lax.broadcasted_iota(jnp.int32, (count, count), 1).astype(F32)
    place = one_hot(turned_rows[:count, 0:1] == nodes)
    copies[2].wait()
    begin = tall_dot(lambda first, last: place[first:last], waves[...]).astype(BF16)
    start[...] = begin
    pick = one_hot(jnp.concatenate([turned_rows[:padded, 1:2], turned_rows[:padded, 2:3]], axis=0) == row)
    one[...] = pick
    copies[3].wait()
    local[...] = tall_dot(lambda first, last: ham[first:last], begin)
    sums[...] = dot(pick, local[...].astype(BF16)).astype(BF16)


def middle_kernel(columns, faces, local, ham, one_t, keep, mine, border):
    count = one_t.shape[0]
    shared = faces.shape[1]
    padded = one_t.shape[1] // 2
    col = columns[:count, 0:1]
    row = faces[...].astype(F32)
    part, parts = lax.axis_index("cells"), lax.axis_size("cells")
    has_before = jnp.where(part > 0, jnp.float32(1), jnp.float32(0))
    has_after = jnp.where(part < parts - 1, jnp.float32(1), jnp.float32(0))
    first = jnp.where(col == row[0:1], jnp.float32(1), jnp.float32(0))
    second = jnp.where(col == row[1:2], jnp.float32(1), jnp.float32(0))
    one_t[...] = jnp.zeros(one_t.shape, BF16)
    one_t[:, :shared] = (first * has_before).astype(BF16)
    one_t[:, padded : padded + shared] = (second * has_after).astype(BF16)
    keep[...] = jnp.broadcast_to(1.0 - jnp.sum(first, axis=1, keepdims=True) * has_before, keep.shape)
    half = (0.5 * local[...]).astype(BF16)
    both = tall_dot(lambda first, last: ham[first:last], jnp.concatenate([half, one_t[...]], axis=1))
    width = local.shape[1]
    mine[...] = both[:, :width]
    border[...] = both[:, width:].astype(BF16)


def second_kernel(before, after, mine, border, start, keep, result, counted, block):
    halo = 0.5 * jnp.concatenate([before[...], after[...]], axis=0).astype(F32)
    sums = mine[...] + tall_dot(lambda first, last: border[first:last], halo.astype(BF16), border.shape[0])
    result[...] = sums
    here = sums - start[...].astype(F32) * keep[...]
    counted[...] = here
    block[...] = here.astype(BF16)


def face_kernel(result, start, one, sums):
    sums[...] = dot(one[...], jnp.concatenate([result[...].astype(BF16), start[...]], axis=1)).astype(BF16)


def third_kernel(counted, before, after, one_t, *rest):
    blocks, gram = rest[:-1], rest[-1]
    width = counted.shape[1]
    here = jnp.concatenate([before[:, :width], after[:, :width]], axis=0)
    there = jnp.concatenate([before[:, width:], jnp.zeros((after.shape[0], width), BF16)], axis=0)
    halo_in = jnp.concatenate([here, there], axis=1)
    halo = tall_dot(lambda first, last: one_t[first:last], halo_in, one_t.shape[0])
    right = (counted[...] + (halo[:, :width] - halo[:, width:])).astype(BF16)
    product = dot_t(right, jnp.concatenate([block[...] for block in blocks], axis=1))
    group = lax.axis_index("bands")
    for at in range(len(blocks)):
        target = 0
        for stride, radix in digits(len(blocks)):
            target = target + (group // stride + at // stride) % radix * stride
        gram[target] = jnp.transpose(product[:, at * width : (at + 1) * width]).astype(BF16)


def vmem(count):
    return [pl.BlockSpec(memory_space=pltpu.VMEM)] * count


def body(wavefunctions, hamiltonians, connectivity, face_nodes):
    node_count, width = wavefunctions.shape
    shared = face_nodes.shape[1]
    padded = -(-shared // 32) * 32
    lanes = -(-node_count // 128) * 128
    parts = lax.axis_size("cells")
    groups = lax.axis_size("bands")
    place = lax.axis_index("cells")
    nodal = (node_count, width)
    shape = jax.ShapeDtypeStruct
    params = pltpu.CompilerParams(vmem_limit_bytes=24 * 2**20)

    start, local, sums, ham, one, columns = pl.pallas_call(
        first_kernel,
        out_shape=(
            shape(nodal, BF16),
            shape(nodal, F32),
            shape((2 * padded, width), BF16),
            shape(hamiltonians.shape[1:], BF16),
            shape((2 * padded, node_count), BF16),
            shape((lanes, 8), F32),
        ),
        in_specs=[pl.BlockSpec(memory_space=pltpu.HBM)] * 4,
        out_specs=tuple(vmem(6)),
        scratch_shapes=[
            pltpu.VMEM(nodal, BF16),
            pltpu.VMEM(connectivity.shape, jnp.int32),
            pltpu.VMEM(face_nodes.shape, jnp.int32),
            pltpu.VMEM((8, lanes), F32),
            pltpu.SemaphoreType.DMA((4,)),
        ],
        compiler_params=params,
    )(*(pltpu.with_memory_space_constraint(x, pltpu.HBM) for x in (wavefunctions, connectivity, face_nodes, hamiltonians)))

    both = ("cells", "bands")
    core, chip = (digits(groups)[0], digits(groups)[-1]) if groups > 1 else ((1, 1), (1, 1))

    def pair_swap(first, spare):
        pairs = []
        for part in range(parts):
            other = first + ((part - first) ^ 1)
            for band in range(groups):
                if part >= first and other < parts:
                    pairs.append((part * groups + band, other * groups + band))
                else:
                    pairs.append((part * groups + band, part * groups + turn(band, *spare, 1)))
        return pairs

    odd = place % 2 == 1
    even = place % 2 == 0

    def neighbours(sums, spare):
        low, high = sums[:padded], sums[padded:]
        even_odd = lax.ppermute(jnp.where(odd, low, high), both, pair_swap(0, spare))
        odd_even = lax.ppermute(jnp.where(odd, high, low), both, pair_swap(1, spare))
        return jnp.where(even, odd_even, even_odd), jnp.where(even, even_odd, odd_even)

    before, after = neighbours(sums, core)
    one_t, keep, mine, border = pl.pallas_call(
        middle_kernel,
        out_shape=(
            shape((node_count, 2 * padded), BF16),
            shape(nodal, F32),
            shape(nodal, F32),
            shape((node_count, 2 * padded), BF16),
        ),
        in_specs=vmem(4),
        out_specs=tuple(vmem(4)),
        compiler_params=params,
    )(columns, face_nodes, local, ham)
    result, counted, block = pl.pallas_call(
        second_kernel,
        out_shape=(shape(nodal, F32), shape(nodal, F32), shape(nodal, BF16)),
        in_specs=vmem(6),
        out_specs=tuple(vmem(3)),
        compiler_params=params,
    )(before, after, mine, border, start, keep)

    blocks = {0: block}
    for stride, radix in reversed(digits(groups)):
        for at in list(blocks):
            for by in range(1, radix):
                blocks[at + by * stride] = lax.ppermute(blocks[at], "bands", turned(groups, stride, radix, radix - by))
    sums = pl.pallas_call(
        face_kernel,
        out_shape=shape((2 * padded, 2 * width), BF16),
        in_specs=vmem(3),
        out_specs=vmem(1)[0],
        compiler_params=params,
    )(result, start, one)
    before, after = neighbours(sums, chip)
    gram = pl.pallas_call(
        third_kernel,
        out_shape=shape((groups, width, width), BF16),
        in_specs=vmem(4 + groups),
        out_specs=vmem(1)[0],
        compiler_params=params,
    )(counted, before, after, one_t, *(blocks[at] for at in range(groups)))
    gram, late_before, late_after = lax.optimization_barrier((gram, before[:, :width], after[:, :width]))
    filtered = result + dot(one_t, jnp.concatenate([late_before, late_after])) - start.astype(F32)
    total = sum_over_cells(gram) * (1.0 / (parts * node_count))
    correlation = total.reshape(groups * width, width)

    place_of = (lax.broadcasted_iota(jnp.int32, (node_count, node_count), 0) == connectivity).astype(BF16)
    top = filtered.astype(BF16)
    rest = filtered - top.astype(F32)
    middle = rest.astype(BF16)
    small = (rest - middle.astype(F32)).astype(BF16)
    return dot(place_of, small) + dot(place_of, middle) + dot(place_of, top), correlation


def solution(mesh):
    placed = (P("cells", "bands"), P("cells", None, None), P("cells", None), P("cells", None))
    return jax.shard_map(
        body,
        mesh=mesh,
        in_specs=placed,
        out_specs=(P("cells", "bands"), P(None, "bands")),
        check_vma=False,
    )
```

```python
import jax
import jax.numpy as jnp
from jax import lax
from jax.experimental import pallas as pl
from jax.experimental.pallas import tpu as pltpu
from jax.sharding import PartitionSpec as P

BF16 = jnp.bfloat16
F32 = jnp.float32


def digits(count):
    stride, left, out = 1, count, []
    for radix in range(2, count + 1):
        while left % radix == 0:
            out.append((stride, radix))
            stride *= radix
            left //= radix
    return out


def turn(index, stride, radix, by):
    digit = index // stride % radix
    return index + ((digit + by) % radix - digit) * stride


def turned(count, stride, radix, by):
    return [(source, turn(source, stride, radix, by)) for source in range(count)]


def sum_over_cells(value):
    parts, groups = lax.axis_size("cells"), lax.axis_size("bands")
    binary = [stride for stride, radix in digits(parts) if radix == 2]
    other = [(stride, radix) for stride, radix in digits(parts) if radix != 2]
    masks = [stride + (stride // 2 if stride > 2 else 0) for stride in binary]
    steps = []
    if len(masks) >= 2:
        first, second = masks[:2]
        steps.append([(first, first ^ second), (second, first), (first ^ second, second)])
        masks = masks[2:]
    steps += [[(mask, mask)] for mask in masks]
    steps = [[lambda part, band, m=m: part ^ m[band % 2] for m in step] for step in steps]
    for stride, radix in other:
        steps.append([lambda part, band, d=(stride, radix, by): turn(part, *d) for by in range(1, radix)])
    kind = BF16 if len(steps) <= 3 else F32
    for step in steps:
        word = value.astype(kind)
        words = [word.astype(F32)]
        for move in step:
            pairs = [
                (part * groups + band, move(part, band) * groups + band) for part in range(parts) for band in range(groups)
            ]
            words.append(lax.ppermute(word, ("cells", "bands"), pairs).astype(F32))
        value = words[0] + words[1]
        if len(words) == 4:
            value = value + (words[2] + words[3])
        elif len(words) == 3:
            value = value + words[2]
    return value


def dot(a, b):
    return jnp.dot(a, b, preferred_element_type=F32)


def dot_t(a, b):
    return lax.dot_general(a, b, (((0,), (0,)), ((), ())), preferred_element_type=F32)


def one_hot(flags):
    return jnp.where(flags, jnp.float32(1), jnp.float32(0)).astype(BF16)


def row_chunks(count):
    return [(first, min(first + 368, count)) for first in range(0, count, 368)]


def tall_dot(rows_of, values, count=None):
    chunks = row_chunks(count or values.shape[0])
    return jnp.concatenate([dot(rows_of(first, last), values) for first, last in chunks], axis=0)


def first_kernel(waves_hbm, cell_hbm, faces_hbm, ham_hbm, start, local, sums, ham, one, columns, waves, cell, faces, rows, sems):
    count = waves.shape[0]
    shared = faces.shape[1]
    padded = one.shape[0] // 2
    pairs = ((cell_hbm, cell), (faces_hbm, faces), (waves_hbm, waves), (ham_hbm.at[0], ham))
    copies = [pltpu.make_async_copy(source, target, sems.at[at]) for at, (source, target) in enumerate(pairs)]
    for copy in copies:
        copy.start()
    rows[...] = jnp.full(rows.shape, -1, F32)
    copies[0].wait()
    copies[1].wait()
    row = cell[...].astype(F32)
    rows[0:1, :count] = row
    rows[1:3, :shared] = faces[...].astype(F32)
    turned_rows = jnp.transpose(rows[...])
    columns[...] = turned_rows
    nodes = lax.broadcasted_iota(jnp.int32, (count, count), 1).astype(F32)
    place = one_hot(turned_rows[:count, 0:1] == nodes)
    copies[2].wait()
    begin = tall_dot(lambda first, last: place[first:last], waves[...]).astype(BF16)
    start[...] = begin
    pick = one_hot(jnp.concatenate([turned_rows[:padded, 1:2], turned_rows[:padded, 2:3]], axis=0) == row)
    one[...] = pick
    copies[3].wait()
    local[...] = tall_dot(lambda first, last: ham[first:last], begin)
    sums[...] = dot(pick, local[...].astype(BF16)).astype(BF16)


def middle_kernel(columns, faces, local, ham, one_t, keep, mine, border):
    count = one_t.shape[0]
    shared = faces.shape[1]
    padded = one_t.shape[1] // 2
    col = columns[:count, 0:1]
    row = faces[...].astype(F32)
    part, parts = lax.axis_index("cells"), lax.axis_size("cells")
    has_before = jnp.where(part > 0, jnp.float32(1), jnp.float32(0))
    has_after = jnp.where(part < parts - 1, jnp.float32(1), jnp.float32(0))
    first = jnp.where(col == row[0:1], jnp.float32(1), jnp.float32(0))
    second = jnp.where(col == row[1:2], jnp.float32(1), jnp.float32(0))
    one_t[...] = jnp.zeros(one_t.shape, BF16)
    one_t[:, :shared] = (first * has_before).astype(BF16)
    one_t[:, padded : padded + shared] = (second * has_after).astype(BF16)
    keep[...] = jnp.broadcast_to(1.0 - jnp.sum(first, axis=1, keepdims=True) * has_before, keep.shape)
    half = (0.5 * local[...]).astype(BF16)
    both = tall_dot(lambda first, last: ham[first:last], jnp.concatenate([half, one_t[...]], axis=1))
    width = local.shape[1]
    mine[...] = both[:, :width]
    border[...] = both[:, width:].astype(BF16)


def second_kernel(before, after, mine, border, start, keep, result, block):
    halo = 0.5 * jnp.concatenate([before[...], after[...]], axis=0).astype(F32)
    sums = mine[...] + tall_dot(lambda first, last: border[first:last], halo.astype(BF16), border.shape[0])
    result[...] = sums
    block[...] = (sums - start[...].astype(F32) * keep[...]).astype(BF16)


def face_kernel(result, start, one, sums):
    sums[...] = dot(one[...], jnp.concatenate([result[...].astype(BF16), start[...]], axis=1)).astype(BF16)


def third_kernel(result, start, keep, before, after, one_t, *rest):
    blocks, (filtered, gram) = rest[:-2], rest[-2:]
    width = result.shape[1]
    here = jnp.concatenate([before[:, :width], after[:, :width]], axis=0)
    there = jnp.concatenate([before[:, width:], jnp.zeros((after.shape[0], width), BF16)], axis=0)
    halo_in = jnp.concatenate([here, there], axis=1)
    halo = tall_dot(lambda first, last: one_t[first:last], halo_in, one_t.shape[0])
    older = start[...].astype(F32)
    whole = result[...] + halo[:, :width]
    filtered[...] = whole - older
    right = (whole - older * keep[...] - halo[:, width:]).astype(BF16)
    product = dot_t(right, jnp.concatenate([block[...] for block in blocks], axis=1))
    group = lax.axis_index("bands")
    for at in range(len(blocks)):
        target = 0
        for stride, radix in digits(len(blocks)):
            target = target + (group // stride + at // stride) % radix * stride
        gram[target] = jnp.transpose(product[:, at * width : (at + 1) * width]).astype(BF16)


def vmem(count):
    return [pl.BlockSpec(memory_space=pltpu.VMEM)] * count


def body(wavefunctions, hamiltonians, connectivity, face_nodes):
    node_count, width = wavefunctions.shape
    shared = face_nodes.shape[1]
    padded = -(-shared // 32) * 32
    lanes = -(-node_count // 128) * 128
    parts = lax.axis_size("cells")
    groups = lax.axis_size("bands")
    place = lax.axis_index("cells")
    nodal = (node_count, width)
    shape = jax.ShapeDtypeStruct
    params = pltpu.CompilerParams(vmem_limit_bytes=24 * 2**20)

    start, local, sums, ham, one, columns = pl.pallas_call(
        first_kernel,
        out_shape=(
            shape(nodal, BF16),
            shape(nodal, F32),
            shape((2 * padded, width), BF16),
            shape(hamiltonians.shape[1:], BF16),
            shape((2 * padded, node_count), BF16),
            shape((lanes, 8), F32),
        ),
        in_specs=[pl.BlockSpec(memory_space=pltpu.HBM)] * 4,
        out_specs=tuple(vmem(6)),
        scratch_shapes=[
            pltpu.VMEM(nodal, BF16),
            pltpu.VMEM(connectivity.shape, jnp.int32),
            pltpu.VMEM(face_nodes.shape, jnp.int32),
            pltpu.VMEM((8, lanes), F32),
            pltpu.SemaphoreType.DMA((4,)),
        ],
        compiler_params=params,
    )(*(pltpu.with_memory_space_constraint(x, pltpu.HBM) for x in (wavefunctions, connectivity, face_nodes, hamiltonians)))

    both = ("cells", "bands")
    chip = digits(groups)[-1] if groups > 1 else (1, 1)

    def pair_swap(first):
        pairs = []
        for part in range(parts):
            other = first + ((part - first) ^ 1)
            for band in range(groups):
                if part >= first and other < parts:
                    pairs.append((part * groups + band, other * groups + band))
                else:
                    pairs.append((part * groups + band, part * groups + turn(band, *chip, 1)))
        return pairs

    odd = place % 2 == 1
    even = place % 2 == 0

    def neighbours(sums):
        low, high = sums[:padded], sums[padded:]
        even_odd = lax.ppermute(jnp.where(odd, low, high), both, pair_swap(0))
        odd_even = lax.ppermute(jnp.where(odd, high, low), both, pair_swap(1))
        return jnp.where(even, odd_even, even_odd), jnp.where(even, even_odd, odd_even)

    before, after = neighbours(sums)
    one_t, keep, mine, border = pl.pallas_call(
        middle_kernel,
        out_shape=(
            shape((node_count, 2 * padded), BF16),
            shape(nodal, F32),
            shape(nodal, F32),
            shape((node_count, 2 * padded), BF16),
        ),
        in_specs=vmem(4),
        out_specs=tuple(vmem(4)),
        compiler_params=params,
    )(columns, face_nodes, local, ham)
    result, block = pl.pallas_call(
        second_kernel,
        out_shape=(shape(nodal, F32), shape(nodal, BF16)),
        in_specs=vmem(6),
        out_specs=tuple(vmem(2)),
        compiler_params=params,
    )(before, after, mine, border, start, keep)

    blocks = {0: block}
    for stride, radix in reversed(digits(groups)):
        for at in list(blocks):
            for by in range(1, radix):
                blocks[at + by * stride] = lax.ppermute(blocks[at], "bands", turned(groups, stride, radix, radix - by))
    sums = pl.pallas_call(
        face_kernel,
        out_shape=shape((2 * padded, 2 * width), BF16),
        in_specs=vmem(3),
        out_specs=vmem(1)[0],
        compiler_params=params,
    )(result, start, one)
    before, after = neighbours(sums)
    filtered, gram = pl.pallas_call(
        third_kernel,
        out_shape=(shape(nodal, F32), shape((groups, width, width), BF16)),
        in_specs=vmem(6 + groups),
        out_specs=tuple(vmem(2)),
        compiler_params=params,
    )(result, start, keep, before, after, one_t, *(blocks[at] for at in range(groups)))
    total = sum_over_cells(gram) * (1.0 / (parts * node_count))
    correlation = total.reshape(groups * width, width)

    place_of = (lax.broadcasted_iota(jnp.int32, (node_count, node_count), 0) == connectivity).astype(BF16)
    top = filtered.astype(BF16)
    rest = filtered - top.astype(F32)
    middle = rest.astype(BF16)
    small = (rest - middle.astype(F32)).astype(BF16)
    return dot(place_of, small) + dot(place_of, middle) + dot(place_of, top), correlation


def solution(mesh):
    placed = (P("cells", "bands"), P("cells", None, None), P("cells", None), P("cells", None))
    return jax.shard_map(
        body,
        mesh=mesh,
        in_specs=placed,
        out_specs=(P("cells", "bands"), P(None, "bands")),
        check_vma=False,
    )
```
